512 devices in a mesh: row: 32 (over x, y, core), col: 16 (over z).
Axes of the slice: x: 4, y: 4, z: 16, core: 2. Of those that a mesh axis runs over, the one named last changes fastest.
Arguments:
- tokens: bfloat16 [4096, 8192], P('row', 'col'), may hold values from -6 to 6
- gate_pre: bfloat16 [4096, 28672], P('col', 'row'), may hold values from -10 to 10
- grad_hidden: bfloat16 [4096, 28672], P('col', 'row'), may hold values from -6 to 6
- up_values: bfloat16 [28672, 8192], P('row', 'col'), may hold values from -0.03125 to 0.03125
- up_scales: float32 [224, 64], P('row', 'col'), may hold values from 0.5 to 2
- adapter_down: float32 [8192, 64], P('col'), may hold values from -0.0625 to 0.0625
- adapter_up: float32 [64, 28672], P(None, 'row'), may hold values from -0.03125 to 0.03125
- layer_gates: float32 [126], replicated, may hold values from 0.25 to 4
- layer: int32 [1], replicated, may hold values from 0 to 125
Outputs:
- grad_input: bfloat16 [4096, 8192], P('row', 'col')
- grad_down: float32 [8192, 64], P('col')
- grad_up: float32 [64, 28672], P(None, 'row')
- gate_grad: float32 [], replicated
The draws below stay inside these ranges and needn't reach their ends.
All inputs are finite; a program needn't handle non-finite values.
Results may differ from the reference program's by a relative error of at most 0.02.
Values may be sent and summed in bfloat16 or wider, within the bound.
A program may use at most 64 MiB of HBM per device.

```python
import math
import jax
import jax.numpy as jnp
from jax import lax

D = 8192
FF = 28672
RANK = 64
QBLOCK = 128
LAYERS = 126
TOKENS = 4096
N_ROW = 32


def level_of(key, extent, shards, low, high):
    factor_of = 1.0
    for axis_at, parts in shards:
        draws = jax.random.uniform(jax.random.fold_in(jax.random.fold_in(key, 6), axis_at), (parts,), jnp.float32, low / len(shards), high / len(shards))
        factor_of = factor_of * jnp.repeat(jnp.exp(draws), extent[axis_at] // parts).reshape((-1,) + (1,) * (len(extent) - 1 - axis_at))
    return factor_of


def scatter_about(key, extent, spread, reach, split=(), kind=jnp.bfloat16):
    level = level_of(key, extent, split, -0.22, 0.18) if split else 1.0
    entries = jax.random.normal(key, extent, jnp.float32) * spread * level
    return jnp.minimum(jnp.maximum(entries, -reach), reach).astype(kind)


def setup_inputs(seed: int = 0) -> dict:
    keys = jax.random.split(jax.random.key(seed), 10)
    return {
        "tokens": scatter_about(keys[0], (TOKENS, D), 1.0, 6.0, ((0, 32), (1, 16))),
        "gate_pre": scatter_about(keys[1], (TOKENS, FF), 2.0, 10.0, ((0, 16), (1, 32))),
        "grad_hidden": scatter_about(keys[2], (TOKENS, FF), 1.0, 6.0, ((0, 16), (1, 32))),
        "up_values": scatter_about(keys[3], (FF, D), FF ** -0.5, 0.03125, ((0, 32), (1, 16))),
        "up_scales": jnp.clip(jnp.exp(math.log(2.0) - 1.3862944 * jax.random.uniform(keys[4], (FF // QBLOCK, D // QBLOCK), jnp.float32) ** level_of(keys[4], (FF // QBLOCK, D // QBLOCK), ((0, 32), (1, 16)), -0.2, 0.2)), 0.5, 2.0),
        "adapter_down": scatter_about(keys[5], (D, RANK), D ** -0.5, 0.0625, ((0, 16),), jnp.float32),
        "adapter_up": scatter_about(keys[6], (RANK, FF), FF ** -0.5, 0.03125, ((1, 32),), jnp.float32),
        "layer_gates": jnp.clip(jnp.exp(jax.random.uniform(keys[7], (LAYERS,), jnp.float32, math.log(0.25), math.log(4.0))), 0.25, 4.0),
        "layer": jax.random.randint(keys[8], (1,), 0, LAYERS).astype(jnp.int32),
    }


def reference(tokens, gate_pre, grad_hidden, up_values, up_scales, adapter_down, adapter_up, layer_gates, layer):
    high = lax.Precision.HIGHEST
    gate_value = jnp.sum(jnp.where(jnp.arange(LAYERS, dtype=jnp.int32) == layer[0], layer_gates, jnp.float32(0.0)))
    grad_pre = (grad_hidden.astype(jnp.float32) * jax.nn.silu(gate_pre.astype(jnp.float32))).astype(jnp.bfloat16)
    expanded = jnp.repeat(jnp.repeat(up_scales, QBLOCK, axis=0), QBLOCK, axis=1)
    weights = (up_values.astype(jnp.float32) * expanded).astype(jnp.bfloat16)
    group = FF // N_ROW
    grad_groups = jnp.transpose(grad_pre.reshape(TOKENS, N_ROW, group), (1, 0, 2))
    weight_groups = weights.reshape(N_ROW, group, D)

    def add_group(total, pair):
        part = jnp.dot(pair[0], pair[1], preferred_element_type=jnp.float32).astype(jnp.bfloat16)
        return total + part.astype(jnp.float32), None

    summed, unused = lax.scan(add_group, jnp.zeros((TOKENS, D), jnp.float32), (grad_groups, weight_groups))
    z_proj = jnp.dot(tokens.astype(jnp.float32), adapter_down, precision=high)
    y_proj = jnp.dot(grad_pre.astype(jnp.float32), adapter_up.T, precision=high)
    grad_input = (summed + gate_value * jnp.dot(y_proj, adapter_down.T, precision=high)).astype(jnp.bfloat16)
    grad_down = gate_value * jnp.dot(tokens.astype(jnp.float32).T, y_proj, precision=high)
    grad_up = gate_value * jnp.dot(z_proj.T, grad_pre.astype(jnp.float32), precision=high)
    gate_grad = jnp.sum(z_proj * y_proj)
    return grad_input, grad_down, grad_up, gate_grad
```

```python
import functools

import jax
import jax.numpy as jnp
from jax import lax
from jax.experimental import pallas as pl
from jax.experimental.pallas import tpu as pltpu
from jax.sharding import PartitionSpec as P

QBLOCK = 128
MESH = pl.DeviceIdType.MESH
F32 = jnp.float32
BF16 = jnp.bfloat16


def split_rows(v):
    high = v.astype(BF16)
    low = (v - high.astype(F32)).astype(BF16)
    return jnp.concatenate([high, low], axis=0)


def fold_rows(v):
    half = v.shape[0] // 2
    return v[:half] + v[half:]


def dot_nt(a, b):
    return lax.dot_general(a, b, (((1,), (1,)), ((), ())), preferred_element_type=F32)


def dot_nn(a, b):
    return jnp.dot(a, b, preferred_element_type=F32)


def kernel(
    n_row,
    n_col,
    tok_ref,
    gate_ref,
    hid_ref,
    up_ref,
    scale_ref,
    down_ref,
    adup_ref,
    gates_ref,
    layer_ref,
    gi_ref,
    gd_ref,
    gu_ref,
    gg_ref,
    gbuf,
    wbuf,
    stage,
    rbuf,
    ost,
    fin,
    lora,
    zst,
    zrb,
    zfull,
    zcat,
    yst,
    yrb,
    y2st,
    yt,
    gst,
    grb,
    gfull,
    sst,
    srb,
    gacc,
    ring_send,
    ring_recv,
    rs_send,
    rs_recv,
    sm_send,
    sm_recv,
):
    r = lax.axis_index("row")
    c = lax.axis_index("col")
    tr, dl = gi_ref.shape
    fl = gbuf.shape[3]
    rank = gd_ref.shape[1]
    n_pc = rank // 8
    half = n_col // 2
    cgs = dl // 128
    Z1, Z2, Z3, Y1, Y2, Y3, D1, D2, S1, FIN = range(10)

    def rcopy(src, dst, ssem, rsem, dev):
        return pltpu.make_async_remote_copy(
            src_ref=src, dst_ref=dst, send_sem=ssem, recv_sem=rsem, device_id=dev, device_id_type=MESH
        )

    def small(src, dst, which, dev):
        return rcopy(src, dst, sm_send.at[which], sm_recv.at[which], dev)

    def plane_peer(i):
        return (lax.rem(r + i, n_row), c)

    def col_peer(i):
        return (r, lax.rem(c + i, n_col))

    def each(low, high, fn):
        def body(i, carry):
            fn(i)
            return carry

        lax.fori_loop(low, high, body, 0)

    barrier = pltpu.get_barrier_semaphore()

    def hello(dev):
        pl.semaphore_signal(barrier, inc=1, device_id=dev, device_id_type=MESH)

    each(1, n_col, lambda i: hello(col_peer(i)))
    each(1, n_row, lambda i: hello(plane_peer(i)))
    even_c = lax.rem(c, 2) == 0
    odd_r = lax.rem(r, 2) == 1
    my_k = c // 2

    @pl.when(even_c)
    def _():
        hello((4 * my_k + 2 * lax.rem(r, 2) + 1, r // 2))

    for h in range(2):
        v = gate_ref[pl.ds(h * tr, tr), :].astype(F32)
        g = hid_ref[pl.ds(h * tr, tr), :].astype(F32) * (v / (1.0 + jnp.exp(-v)))
        gbuf[c, h] = g.astype(BF16)

    @pl.when(odd_r)
    def _():
        pl.semaphore_wait(barrier, n_col + n_row - 1)

    @pl.when(jnp.logical_not(odd_r))
    def _():
        pl.semaphore_wait(barrier, n_col + n_row - 2)

    right = lax.rem(c + 1, n_col)
    left = lax.rem(c + n_col - 1, n_col)

    def ring(way, s, h):
        if way == 0:
            block, dev = lax.rem(c - s + n_col, n_col), (r, right)
        else:
            block, dev = lax.rem(c + s, n_col), (r, left)
        part = gbuf.at[block, h]
        return rcopy(part, part, ring_send.at[way, s, h], ring_recv.at[way, s, h], dev)

    for h in range(2):
        for way in range(2):
            ring(way, 0, h).start()

    gv = gates_ref[layer_ref[0]]
    a_t = down_ref[...].T
    zst[...] = fold_rows(dot_nt(split_rows(a_t), tok_ref[...])).reshape(n_pc, 8, tr)

    def z1(k):
        @pl.when(2 * k != c)
        def _():
            small(zst.at[k], zrb.at[c], Z1, (r, 2 * k)).start()

    each(0, n_pc, z1)

    own = gbuf[c].reshape(2 * tr, fl)
    y_part = fold_rows(dot_nt(split_rows(adup_ref[...]), own))
    for k in range(n_pc):
        for h in range(2):
            yst[2 * k + h] = y_part[8 * k : 8 * k + 8, h * tr : (h + 1) * tr]

    def y1(i):
        @pl.when(2 * i + 1 != r)
        def _():
            small(yst.at[i], yrb.at[r], Y1, (2 * i + 1, c)).start()

    each(0, 2 * n_pc, y1)

    for i in range(fl // QBLOCK):
        for j in range(dl // QBLOCK):
            at = (pl.ds(i * QBLOCK, QBLOCK), pl.ds(j * QBLOCK, QBLOCK))
            wbuf[at] = (up_ref[at].astype(F32) * scale_ref[i, j]).astype(BF16)

    def multiply(block, group, at):
        p = dot_nn(gbuf[block].reshape(2 * tr, fl), wbuf[...]).astype(BF16)
        for h in range(2):
            for tg in range(tr // 16):
                for cg in range(cgs):
                    stage[group, tg * cgs + cg, at + h] = p[
                        h * tr + 16 * tg : h * tr + 16 * tg + 16, 128 * cg : 128 * cg + 128
                    ]

    def scatter(group, parts):
        def send(i):
            j = lax.rem(r + i, n_row)
            rcopy(
                stage.at[group, j, pl.ds(0, parts)],
                rbuf.at[group, r, pl.ds(0, parts)],
                rs_send.at[group],
                rs_recv.at[group],
                (j, c),
            ).start()

        each(1, n_row, send)
        rbuf[group, r, pl.ds(0, parts)] = stage[group, r, pl.ds(0, parts)]

    def reduce(group, parts, blocks):
        got = rbuf.at[group, pl.ds(0, n_row - 1), pl.ds(0, parts)]
        rcopy(got, got, rs_send.at[group], rs_recv.at[group], (r, right)).wait_recv()

        def add(i, acc):
            return acc + rbuf[group, i, pl.ds(0, parts)].astype(F32)

        total = lax.fori_loop(0, n_row, add, jnp.zeros((parts, 16, 128), F32))
        ost[group, pl.ds(0, parts)] = total.astype(BF16)
        for part in range(parts):
            dest = 2 * blocks[part // 2] + part % 2

            @pl.when(dest != r)
            def _():
                small(ost.at[group, part], fin.at[r], FIN, (dest, c)).start()

            @pl.when(dest == r)
            def _():
                fin[r] = ost[group, part]

    def blocks_of(s):
        return (lax.rem(c - s + n_col, n_col), lax.rem(c + s, n_col))

    multiply(c, 0, 0)
    scatter(0, 2)

    def wait_small(which, ref):
        small(ref, ref, which, (r, right)).wait_recv()

    def hook_z1_y1():
        @pl.when(even_c)
        def _():
            zrb[c] = zst[my_k]
            wait_small(Z1, zrb.at[pl.ds(0, n_col - 1)])
            zfull[r, my_k] = jnp.sum(zrb[...], axis=0)
            each(1, n_col, lambda i: small(zfull.at[r, my_k], zfull.at[r, my_k], Z2, col_peer(i)).start())

        @pl.when(odd_r)
        def _():
            i = r // 2
            yrb[r] = yst[i]
            wait_small(Y1, yrb.at[pl.ds(0, n_row - 1)])
            y2st[...] = jnp.sum(yrb[...], axis=0)
            k = i // 2
            small(y2st, yt.at[k], Y2, (2 * c + lax.rem(i, 2), 2 * k)).start()

    def wait_pieces(which, ref):
        @pl.when(even_c)
        def _():
            if n_pc > 1:
                wait_small(which, ref.at[pl.ds(0, n_pc - 1)])

        @pl.when(jnp.logical_not(even_c))
        def _():
            wait_small(which, ref.at[pl.ds(0, n_pc)])

    def hook_z2_y2():
        wait_pieces(Z2, zfull.at[r])
        each(1, n_row, lambda i: small(zfull.at[r], zfull.at[r], Z3, plane_peer(i)).start())

        @pl.when(even_c)
        def _():
            wait_small(Y2, yt.at[my_k])
            each(1, n_col, lambda i: small(yt.at[my_k], yt.at[my_k], Y3, col_peer(i)).start())

    def hook_y3():
        wait_pieces(Y3, yt)
        y_t = yt[...].reshape(rank, tr)
        gd_t = fold_rows(dot_nn(split_rows(y_t), tok_ref[...]))
        for k in range(n_pc):
            for q in range(cgs):
                gst[k * cgs + q] = gd_t[8 * k : 8 * k + 8, 128 * q : 128 * q + 128]

        def send(i):
            j = lax.rem(r + i, n_row)
            small(gst.at[j], grb.at[r], D1, (j, c)).start()

        each(1, n_row, send)
        grb[r] = gst[r]

    def hook_lora():
        y_s = split_rows(yt[...].reshape(rank, tr))
        a_s = split_rows(down_ref[...].T)
        y_left = jnp.concatenate([y_s[:rank], y_s[:rank], y_s[rank:]], axis=0).astype(F32).T.astype(BF16)
        a_right = jnp.concatenate([a_s[:rank], a_s[rank:], a_s[:rank]], axis=0)
        lora[...] = gv * dot_nn(y_left, a_right)

    def hook_d1():
        wait_small(D1, grb.at[pl.ds(0, n_row - 1)])
        gfull[r] = jnp.sum(grb[...], axis=0)
        each(1, n_row, lambda i: small(gfull.at[r], gfull.at[r], D2, plane_peer(i)).start())

    def hook_d2():
        wait_small(D2, gfull.at[pl.ds(0, n_row - 1)])
        rows = []
        for k in range(n_pc):
            rows.append(jnp.concatenate([gfull[k * cgs + q] for q in range(cgs)], axis=1))
        gd_t = jnp.concatenate(rows, axis=0)
        gd_ref[...] = gv * gd_t.T
        total = jnp.sum(gd_t * down_ref[...].T)
        sst[...] = jnp.full(sst.shape, total, F32)
        srb[c] = sst[...]
        each(1, n_col, lambda i: small(sst, srb.at[c], S1, col_peer(i)).start())

    def hook_z3():
        wait_small(Z3, zfull.at[pl.ds(0, n_row - 1)])

        def one(b):
            z_t = jnp.concatenate(
                [zfull[2 * b].reshape(rank, tr), zfull[2 * b + 1].reshape(rank, tr)], axis=1
            )
            zcat[b] = split_rows(z_t)

        each(0, n_col, one)

    def hook_s1():
        wait_small(S1, srb.at[pl.ds(0, n_col - 1)])
        gg_ref[0, 0] = jnp.sum(jnp.sum(srb[...], axis=0)[0:1, 0:1])

    hooks = [
        (hook_z1_y1,),
        (hook_z2_y2,),
        (hook_y3,),
        (hook_d1, hook_lora),
        (hook_d2,),
        (hook_z3,),
        (hook_s1,),
    ]

    def step(s):
        ups, downs = blocks_of(s)

        for way in range(2):
            ring(way, s - 1, 0).wait_recv()
            if way == 0:
                ring(way, s, 0).start()
            else:
                pl.when(s < half - 1)(lambda: ring(1, s, 0).start())

        before = blocks_of(s - 1)

        @pl.when(s == 1)
        def _():
            reduce(0, 2, (c,))

        @pl.when(s > 1)
        def _():
            reduce(s - 1, 4, before)

        for at, some in enumerate(hooks):
            if at + 1 < half:

                @pl.when(s == at + 1)
                def _():
                    for hook in some:
                        hook()

        for way in range(2):
            ring(way, s - 1, 1).wait_recv()
            if way == 1:
                ring(way, s, 1).start()
            else:
                pl.when(s < half - 1)(lambda: ring(0, s, 1).start())

        multiply(ups, s, 0)
        multiply(downs, s, 2)
        scatter(s, 4)

    each(1, half, step)
    for at, some in enumerate(hooks):
        if at + 1 >= half:
            for hook in some:
                hook()

    reduce(half - 1, 4, blocks_of(half - 1))
    far = lax.rem(c + half, n_col)
    ring(0, half - 1, 0).wait_recv()
    ring(1, half - 1, 1).wait_recv()
    multiply(far, half, 0)
    scatter(half, 2)

    gacc[...] = jnp.zeros_like(gacc)

    def up_block(b):
        gacc[...] += dot_nn(zcat[b], gbuf[b].reshape(2 * tr, fl))

    each(0, n_col, up_block)
    gu_ref[...] = gv * fold_rows(gacc[...])

    reduce(half, 2, (far,))
    wait_small(FIN, fin.at[pl.ds(0, n_row - 1)])
    for tg in range(tr // 16):
        for cg in range(cgs):
            at = (pl.ds(16 * tg, 16), pl.ds(128 * cg, 128))
            gi_ref[at] = (fin[tg * cgs + cg].astype(F32) + lora[at]).astype(BF16)

    def drain(s):
        for way in range(2):
            for h in range(2):
                if way == h:
                    ring(way, s, h).wait_send()
                else:
                    pl.when(s < half - 1)(lambda: ring(way, s, h).wait_send())

    each(0, half, drain)

    def sent_group(group, parts):
        out = stage.at[group, pl.ds(0, n_row - 1), pl.ds(0, parts)]
        rcopy(out, out, rs_send.at[group], rs_recv.at[group], (r, right)).wait_send()

    sent_group(0, 2)
    each(1, half, lambda s: sent_group(s, 4))
    sent_group(half, 2)

    def sent(which, ref):
        small(ref, ref, which, (r, right)).wait_send()

    @pl.when(even_c)
    def _():
        if n_pc > 1:
            sent(Z1, zst.at[pl.ds(0, n_pc - 1)])
        sent(Z2, zrb.at[pl.ds(0, n_col - 1)])
        sent(Y3, zrb.at[pl.ds(0, n_col - 1)])

    @pl.when(jnp.logical_not(even_c))
    def _():
        sent(Z1, zst)

    @pl.when(odd_r)
    def _():
        sent(Y1, yst.at[pl.ds(0, 2 * n_pc - 1)])
        sent(Y2, y2st)

    @pl.when(jnp.logical_not(odd_r))
    def _():
        sent(Y1, yst)

    sent(Z3, zfull.at[pl.ds(0, n_row - 1)])
    sent(D1, gst.at[pl.ds(0, n_row - 1)])
    sent(D2, gfull.at[pl.ds(0, n_row - 1)])
    sent(S1, srb.at[pl.ds(0, n_col - 1)])
    sent(FIN, fin.at[pl.ds(0, 2 * n_col - 1)])


def per_device(
    n_row,
    n_col,
    tokens,
    gate_pre,
    grad_hidden,
    up_values,
    up_scales,
    adapter_down,
    adapter_up,
    layer_gates,
    layer,
):
    tr, dl = tokens.shape
    fl = up_values.shape[0]
    rank = adapter_down.shape[1]
    n_pc = rank // 8
    groups = n_col // 2 + 1
    vmem = pl.BlockSpec(memory_space=pltpu.VMEM)
    smem = pl.BlockSpec(memory_space=pltpu.SMEM)
    outs = pl.pallas_call(
        functools.partial(kernel, n_row, n_col),
        out_shape=(
            jax.ShapeDtypeStruct((tr, dl), BF16),
            jax.ShapeDtypeStruct((dl, rank), F32),
            jax.ShapeDtypeStruct((rank, fl), F32),
            jax.ShapeDtypeStruct((1, 1), F32),
        ),
        in_specs=[vmem, vmem, vmem, vmem, smem, vmem, vmem, smem, smem],
        out_specs=(vmem, vmem, vmem, smem),
        scratch_shapes=[
            pltpu.VMEM((n_col, 2, tr, fl), BF16),
            pltpu.VMEM((fl, dl), BF16),
            pltpu.VMEM((groups, n_row, 4, 16, 128), BF16),
            pltpu.VMEM((groups, n_row, 4, 16, 128), BF16),
            pltpu.VMEM((groups, 4, 16, 128), BF16),
            pltpu.VMEM((n_row, 16, 128), BF16),
            pltpu.VMEM((tr, dl), F32),
            pltpu.VMEM((n_pc, 8, tr), F32),
            pltpu.VMEM((n_col, 8, tr), F32),
            pltpu.VMEM((n_row, n_pc, 8, tr), F32),
            pltpu.VMEM((n_col, 2 * rank, 2 * tr), BF16),
            pltpu.VMEM((2 * n_pc, 8, tr), F32),
            pltpu.VMEM((n_row, 8, tr), F32),
            pltpu.VMEM((8, tr), F32),
            pltpu.VMEM((n_pc, 8, tr), F32),
            pltpu.VMEM((n_row, 8, 128), F32),
            pltpu.VMEM((n_row, 8, 128), F32),
            pltpu.VMEM((n_row, 8, 128), F32),
            pltpu.VMEM((8, 128), F32),
            pltpu.VMEM((n_col, 8, 128), F32),
            pltpu.VMEM((2 * rank, fl), F32),
            pltpu.SemaphoreType.DMA((2, n_col // 2, 2)),
            pltpu.SemaphoreType.DMA((2, n_col // 2, 2)),
            pltpu.SemaphoreType.DMA((groups,)),
            pltpu.SemaphoreType.DMA((groups,)),
            pltpu.SemaphoreType.DMA((10,)),
            pltpu.SemaphoreType.DMA((10,)),
        ],
        compiler_params=pltpu.CompilerParams(
            collective_id=0, has_side_effects=True, vmem_limit_bytes=48 * 1024 * 1024
        ),
    )(
        tokens,
        gate_pre,
        grad_hidden,
        up_values,
        up_scales,
        adapter_down,
        adapter_up,
        layer_gates,
        layer,
    )
    grad_input, grad_down, grad_up, gate_grad = outs
    return grad_input, grad_down, grad_up, gate_grad.reshape(())


def solution(mesh):
    placed = (
        P("row", "col"),
        P("col", "row"),
        P("col", "row"),
        P("row", "col"),
        P("row", "col"),
        P("col", None),
        P(None, "row"),
        P(),
        P(),
    )
    return jax.shard_map(
        functools.partial(per_device, mesh.shape["row"], mesh.shape["col"]),
        mesh=mesh,
        in_specs=placed,
        out_specs=(P("row", "col"), P("col", None), P(None, "row"), P()),
        check_vma=False,
    )
```

```python
import functools

import jax
import jax.numpy as jnp
from jax import lax
from jax.experimental import pallas as pl
from jax.experimental.pallas import tpu as pltpu
from jax.sharding import PartitionSpec as P

QBLOCK = 128
SUB = 4
MESH = pl.DeviceIdType.MESH
F32 = jnp.float32
BF16 = jnp.bfloat16
Z1, Z2, Z3, Y1, Y2, Y3, D1, D2, S1, FIN = range(10)


def split_rows(v):
    high = v.astype(BF16)
    low = (v - high.astype(F32)).astype(BF16)
    return jnp.concatenate([high, low], axis=0)


def fold_rows(v):
    half = v.shape[0] // 2
    return v[:half] + v[half:]


def dot_nt(a, b):
    return lax.dot_general(a, b, (((1,), (1,)), ((), ())), preferred_element_type=F32)


def dot_nn(a, b):
    return jnp.dot(a, b, preferred_element_type=F32)


def each(low, high, fn):
    def body(i, carry):
        fn(i)
        return carry

    lax.fori_loop(low, high, body, 0)


def kernel(
    n_row,
    n_col,
    tok_hbm,
    gate_hbm,
    hid_hbm,
    up_hbm,
    scale_ref,
    down_hbm,
    adup_hbm,
    gates_ref,
    layer_ref,
    gi_ref,
    gd_ref,
    gu_ref,
    gg_ref,
    tok,
    gate,
    hid,
    up,
    a_t,
    adup,
    gbuf,
    wbuf,
    keep,
    xst,
    xrb,
    stage,
    rbuf,
    ost,
    fin,
    lora,
    zst,
    zrb,
    zfull,
    zcat,
    gpart,
    yst,
    yrb,
    y2st,
    yt,
    gst,
    grb,
    gfull,
    srb,
    load_sem,
    ring_send,
    ring_recv,
    x_send,
    x_recv,
    rs_send,
    rs_recv,
    sm_send,
    sm_recv,
):
    r = lax.axis_index("row")
    c = lax.axis_index("col")
    core = lax.rem(r, 2)
    chip = lax.div(r, 2)
    tr, dl = gi_ref.shape
    fl = wbuf.shape[0]
    rank = gd_ref.shape[0]
    sub = 2 * tr // SUB
    n_pc = rank // 8
    n_chip = n_row // 2
    half = n_col // 2
    cgs = dl // 128
    tgs = n_chip // cgs
    right = lax.rem(c + 1, n_col)
    left = lax.rem(c + n_col - 1, n_col)
    odd = core == 1
    n_zp = rank // 16
    z_gap = n_col // n_zp
    z_owner = lax.rem(c, z_gap) == 0
    y_owner = lax.rem(c, 2) == 0
    my_z, my_k = lax.div(c, z_gap), lax.div(c, 2)

    def rcopy(src, dst, ssem, rsem, dev):
        return pltpu.make_async_remote_copy(
            src_ref=src, dst_ref=dst, send_sem=ssem, recv_sem=rsem, device_id=dev, device_id_type=MESH
        )

    def small(src, dst, which, dev):
        return rcopy(src, dst, sm_send.at[which], sm_recv.at[which], dev)

    def wait_small(which, ref):
        small(ref, ref, which, (r, right)).wait_recv()

    def sent(which, ref):
        small(ref, ref, which, (r, right)).wait_send()

    def plane_peer(i):
        return (lax.rem(r + i, n_row), c)

    def col_peer(i):
        return (r, lax.rem(c + i, n_col))

    barrier = pltpu.get_barrier_semaphore()

    def hello(dev):
        pl.semaphore_signal(barrier, inc=1, device_id=dev, device_id_type=MESH)

    each(1, n_col, lambda i: hello(col_peer(i)))
    pl.when(y_owner)(lambda: hello((4 * my_k + 2 * core + 1, chip)))
    each(1, n_row, lambda i: hello(plane_peer(i)))

    def rows(q):
        return pl.ds(q * sub, sub)

    loads = []
    for q in range(SUB):
        for at, (src, dst) in enumerate(((gate_hbm, gate), (hid_hbm, hid))):
            loads.append(pltpu.make_async_copy(src.at[rows(q)], dst.at[rows(q)], load_sem.at[2 * q + at]))
    for at, (src, dst) in enumerate(((tok_hbm, tok), (down_hbm, a_t), (adup_hbm, adup), (up_hbm, up))):
        loads.append(pltpu.make_async_copy(src, dst, load_sem.at[2 * SUB + at]))
    for load in loads:
        load.start()

    def ring(way, s, h):
        if way == 0:
            block, dev = lax.rem(c - s + n_col, n_col), (r, right)
        else:
            block, dev = lax.rem(c + s, n_col), (r, left)
        part = gbuf.at[block, h]
        return rcopy(part, part, ring_send.at[way, s, h], ring_recv.at[way, s, h], dev)

    for q in range(SUB):
        loads[2 * q].wait()
        loads[2 * q + 1].wait()
        v = gate[rows(q), :].astype(F32)
        gbuf[c, q] = (hid[rows(q), :].astype(F32) * (v / (1.0 + jnp.exp(-v)))).astype(BF16)
        if q == 0:
            pl.when(odd)(lambda: pl.semaphore_wait(barrier, n_col + n_row - 1))
            pl.when(jnp.logical_not(odd))(lambda: pl.semaphore_wait(barrier, n_col + n_row - 2))
        for way in range(2):
            ring(way, 0, q).start()

    gv = gates_ref[layer_ref[0]]
    for load in loads[2 * SUB :]:
        load.wait()

    zst[...] = fold_rows(dot_nt(split_rows(a_t[...]), tok[...])).astype(BF16).reshape(n_zp, 16, tr)

    def z1(k):
        @pl.when(z_gap * k != c)
        def _():
            small(zst.at[k], zrb.at[c], Z1, (r, z_gap * k)).start()

    each(0, n_zp, z1)
    y_part = fold_rows(dot_nt(split_rows(adup[...]), gbuf[c].reshape(2 * tr, fl)))
    for k in range(n_pc):
        for h in range(2):
            yst[2 * k + h] = y_part[8 * k : 8 * k + 8, h * tr : (h + 1) * tr]

    def y1(i):
        @pl.when(2 * i + 1 != r)
        def _():
            small(yst.at[i], yrb.at[r], Y1, (2 * i + 1, c)).start()

    each(0, 2 * n_pc, y1)

    def blocks_of(s):
        return (lax.rem(c - s + n_col, n_col), lax.rem(c + s, n_col))

    def tiles(v, put):
        for t in range(v.shape[0] // 16):
            for cg in range(cgs):
                put((t % tgs) * cgs + cg, t // tgs, v[16 * t : 16 * t + 16, 128 * cg : 128 * cg + 128])

    def multiply(group, parts, ours, theirs):
        def put_theirs(owner, at, v):
            xst[group, owner, at] = v.astype(BF16)

        def put_ours(owner, at, v):
            keep[owner, at] = v

        tiles(dot_nn(theirs, wbuf[...]), put_theirs)
        out, into = xst.at[group, :, pl.ds(0, parts)], xrb.at[group, :, pl.ds(0, parts)]
        rcopy(out, into, x_send.at[group], x_recv.at[group], (r + 1 - 2 * core, c)).start()
        tiles(dot_nn(ours, wbuf[...]), put_ours)

    def halves(block):
        def one(h):
            return jnp.concatenate([gbuf[block, 2 * h], gbuf[block, 2 * h + 1]], axis=0)

        return one(core), one(1 - core)

    def multiply_pair(s):
        ups, downs = blocks_of(s)
        up_ours, up_theirs = halves(ups)
        down_ours, down_theirs = halves(downs)
        multiply(
            s,
            4,
            jnp.concatenate([up_ours, down_ours], axis=0),
            jnp.concatenate([up_theirs, down_theirs], axis=0),
        )

    def scatter(group, parts):
        into = xrb.at[group, :, pl.ds(0, parts)]
        rcopy(into, into, x_send.at[group], x_recv.at[group], (r + 1 - 2 * core, c)).wait_recv()

        def add(p):
            both = keep[p, pl.ds(0, parts)] + xrb[group, p, pl.ds(0, parts)].astype(F32)
            stage[group, p, pl.ds(0, parts)] = both.astype(BF16)

        each(0, n_chip, add)

        def send(i):
            p = lax.rem(chip + i, n_chip)
            rcopy(
                stage.at[group, p, pl.ds(0, parts)],
                rbuf.at[group, chip, pl.ds(0, parts)],
                rs_send.at[group],
                rs_recv.at[group],
                (2 * p + core, c),
            ).start()

        each(1, n_chip, send)
        rbuf[group, chip, pl.ds(0, parts)] = stage[group, chip, pl.ds(0, parts)]

    def reduce(group, parts, pieces):
        got = rbuf.at[group, pl.ds(0, n_chip - 1), pl.ds(0, parts)]
        rcopy(got, got, rs_send.at[group], rs_recv.at[group], (r, right)).wait_recv()

        def add(i, acc):
            return acc + rbuf[group, i, pl.ds(0, parts)].astype(F32)

        total = lax.fori_loop(0, n_chip, add, jnp.zeros((parts, 16, 128), F32))
        ost[group, pl.ds(0, parts)] = total.astype(BF16)
        for at, size, block, place in pieces:

            @pl.when(block != chip)
            def _():
                small(
                    ost.at[group, pl.ds(at, size)],
                    fin.at[chip, pl.ds(place, size)],
                    FIN,
                    (2 * block + core, c),
                ).start()

            @pl.when(block == chip)
            def _():
                fin[chip, pl.ds(place, size)] = ost[group, pl.ds(at, size)]

    def reduce_pair(s):
        ups, downs = blocks_of(s)
        reduce(s, 4, ((0, 2, ups, 0), (2, 2, downs, 0)))

    def weights_and_own():
        for i in range(fl // QBLOCK):
            for j in range(dl // QBLOCK):
                at = (pl.ds(i * QBLOCK, QBLOCK), pl.ds(j * QBLOCK, QBLOCK))
                wbuf[at] = (up[at].astype(F32) * scale_ref[j, i]).astype(BF16)
        ours, theirs = halves(c)
        multiply(0, 2, ours, theirs)

    def to_column(ref, which):
        each(1, n_col, lambda i: small(ref, ref, which, col_peer(i)).start())

    def wait_pieces(which, owner, count, ref):
        @pl.when(owner)
        def _():
            if count > 1:
                wait_small(which, ref.at[pl.ds(0, count - 1)])

        pl.when(jnp.logical_not(owner))(lambda: wait_small(which, ref))

    def z_sum():
        @pl.when(z_owner)
        def _():
            zrb[c] = zst[my_z]
            wait_small(Z1, zrb.at[pl.ds(0, n_col - 1)])
            zfull[r, my_z] = jnp.sum(zrb[...].astype(F32), axis=0).astype(BF16)
            to_column(zfull.at[r, my_z], Z2)

    def z_plane():
        wait_pieces(Z2, z_owner, n_zp, zfull.at[r])
        each(1, n_row, lambda i: small(zfull.at[r], zfull.at[r], Z3, plane_peer(i)).start())

    def z_ready():
        wait_small(Z3, zfull.at[pl.ds(0, n_row - 1)])

        def join(b):
            zcat[b] = jnp.concatenate(
                [zfull[2 * b].reshape(rank, tr), zfull[2 * b + 1].reshape(rank, tr)], axis=1
            )

        each(0, n_col, join)

    def y_sum():
        @pl.when(odd)
        def _():
            yrb[r] = yst[chip]
            wait_small(Y1, yrb.at[pl.ds(0, n_row - 1)])
            y2st[...] = jnp.sum(yrb[...], axis=0)
            k = lax.div(chip, 2)
            small(y2st, yt.at[k], Y2, (2 * c + lax.rem(chip, 2), 2 * k)).start()

    def y_column():
        @pl.when(y_owner)
        def _():
            wait_small(Y2, yt.at[my_k])
            to_column(yt.at[my_k], Y3)

    def up_block(b):
        gpart[b] = dot_nn(zcat[b], gbuf[b].reshape(2 * tr, fl))

    def down_part():
        wait_pieces(Y3, y_owner, n_pc, yt)
        gd_t = fold_rows(dot_nn(split_rows(yt[...].reshape(rank, tr)), tok[...]))
        for k in range(n_pc):
            for q in range(cgs):
                gst[k * cgs + q] = gd_t[8 * k : 8 * k + 8, 128 * q : 128 * q + 128]

        def send(i):
            j = lax.rem(r + i, n_row)
            small(gst.at[j], grb.at[r], D1, (j, c)).start()

        each(1, n_row, send)
        grb[r] = gst[r]

    def make_lora():
        y_s = split_rows(yt[...].reshape(rank, tr))
        a_s = split_rows(a_t[...])
        y_left = jnp.concatenate([y_s[:rank], y_s[:rank], y_s[rank:]], axis=0).astype(F32).T.astype(BF16)
        a_right = jnp.concatenate([a_s[:rank], a_s[rank:], a_s[:rank]], axis=0)
        lora[...] = gv * dot_nn(y_left, a_right)

    def down_sum():
        wait_small(D1, grb.at[pl.ds(0, n_row - 1)])
        gfull[r] = jnp.sum(grb[...], axis=0)
        each(1, n_row, lambda i: small(gfull.at[r], gfull.at[r], D2, plane_peer(i)).start())

    def down_ready():
        wait_small(D2, gfull.at[pl.ds(0, n_row - 1)])
        strips = []
        for k in range(n_pc):
            strips.append(jnp.concatenate([gfull[k * cgs + q] for q in range(cgs)], axis=1))
        gd_t = jnp.concatenate(strips, axis=0)
        gd_ref[...] = gv * gd_t
        srb[c] = jnp.full(srb.shape[1:], jnp.sum(gd_t * a_t[...]), F32)

        to_column_gate()

    def to_column_gate():
        each(1, n_col, lambda i: small(srb.at[c], srb.at[c], S1, col_peer(i)).start())

    def gate_done():
        wait_small(S1, srb.at[pl.ds(0, n_col - 1)])
        gg_ref[0, 0] = jnp.sum(jnp.sum(srb[...], axis=0)[:, 0:1])

    up_at = 20

    def work(n):
        s, h = 1 + lax.div(n, SUB), lax.rem(n, SUB)
        pl.when(n == 0)(weights_and_own)
        @pl.when(jnp.logical_and(h == 1, s < half))
        def _():
            pl.when(s == 1)(lambda: scatter(0, 2))
            pl.when(s > 1)(lambda: scatter(s - 1, 4))

        @pl.when(jnp.logical_and(h == 3, s < half))
        def _():
            multiply_pair(s)
            pl.when(s == 1)(lambda: reduce(0, 2, ((0, 2, c, 0),)))
            pl.when(s > 1)(lambda: reduce_pair(s - 1))

        pl.when(n == 3)(y_sum)
        pl.when(n == 6)(z_sum)
        pl.when(n == 8)(y_column)
        pl.when(n == 11)(z_plane)
        pl.when(n == 13)(down_part)
        pl.when(n == 14)(make_lora)
        pl.when(n == 15)(z_ready)
        pl.when(n == 16)(down_sum)
        pl.when(n == 18)(down_ready)
        pl.when(n == 26)(gate_done)

        @pl.when(jnp.logical_and(n >= up_at, n < up_at + half))
        def _():
            ups, downs = blocks_of(n - up_at)
            up_block(ups)
            pl.when(n > up_at)(lambda: up_block(downs))

    def slot(n):
        s, h = 1 + lax.div(n, SUB), lax.rem(n, SUB)
        ring(0, s - 1, h).wait_recv()
        pl.when(jnp.logical_or(s < half - 1, h < SUB // 2))(lambda: ring(0, s, h).start())
        ring(1, s - 1, h).wait_recv()
        pl.when(jnp.logical_or(s < half - 1, h >= SUB // 2))(lambda: ring(1, s, h).start())
        work(n)

    slots = SUB * (half - 1)
    each(0, slots, slot)
    last = up_at + 8
    if last > slots:
        each(slots, last, work)

    far = lax.rem(c + half, n_col)
    scatter(half - 1, 4)
    for t in range(2):
        ring(0, half - 1, t).wait_recv()
        ring(1, half - 1, t + 2).wait_recv()
        multiply(half + t, 1, gbuf[far, 2 * core + t], gbuf[far, 2 - 2 * core + t])
        scatter(half + t, 1)
    up_block(far)
    reduce_pair(half - 1)
    reduce(half, 1, ((0, 1, far, 0),))
    acc = gpart[0]
    for b in range(1, n_col):
        acc = acc + gpart[b]
    gu_ref[...] = gv * acc
    reduce(half + 1, 1, ((0, 1, far, 1),))
    wait_small(FIN, fin.at[pl.ds(0, n_chip - 1)])
    for p in range(n_chip):
        for at in range(2):
            here = (pl.ds(16 * (tgs * at + p // cgs), 16), pl.ds(128 * (p % cgs), 128))
            gi_ref[here] = (fin[p, at].astype(F32) + lora[here]).astype(BF16)

    def drain(s):
        for way in range(2):
            for h in range(SUB):
                if (way == 0) == (h < SUB // 2):
                    ring(way, s, h).wait_send()
                else:
                    pl.when(s < half - 1)(lambda: ring(way, s, h).wait_send())

    each(0, half, drain)

    def sent_group(group, parts):
        out = xst.at[group, :, pl.ds(0, parts)]
        rcopy(out, out, x_send.at[group], x_recv.at[group], (r, right)).wait_send()
        out = stage.at[group, pl.ds(0, n_chip - 1), pl.ds(0, parts)]
        rcopy(out, out, rs_send.at[group], rs_recv.at[group], (r, right)).wait_send()

    sent_group(0, 2)
    each(1, half, lambda s: sent_group(s, 4))
    sent_group(half, 1)
    sent_group(half + 1, 1)

    @pl.when(odd)
    def _():
        sent(Y1, yst.at[pl.ds(0, 2 * n_pc - 1)])
        sent(Y2, y2st)

    pl.when(jnp.logical_not(odd))(lambda: sent(Y1, yst))

    @pl.when(z_owner)
    def _():
        if n_zp > 1:
            sent(Z1, zst.at[pl.ds(0, n_zp - 1)])
        sent(Z2, zrb.at[pl.ds(0, n_col - 1)])

    pl.when(jnp.logical_not(z_owner))(lambda: sent(Z1, zst))
    pl.when(y_owner)(lambda: sent(Y3, yrb.at[pl.ds(0, n_col - 1)]))
    sent(S1, srb.at[pl.ds(0, n_col - 1)])
    sent(Z3, zfull.at[pl.ds(0, n_row - 1)])
    sent(D1, gst.at[pl.ds(0, n_row - 1)])
    sent(D2, gfull.at[pl.ds(0, n_row - 1)])
    sent(FIN, fin.at[pl.ds(0, n_chip - 1)])


def per_device(
    n_row,
    n_col,
    tokens,
    gate_pre,
    grad_hidden,
    up_values,
    up_scales,
    adapter_down,
    adapter_up,
    layer_gates,
    layer,
):
    tr, dl = tokens.shape
    fl = up_values.shape[0]
    rank = adapter_down.shape[1]
    n_pc = rank // 8
    n_chip = n_row // 2
    half = n_col // 2
    groups = half + 2
    hbm = pl.BlockSpec(memory_space=pltpu.HBM)
    vmem = pl.BlockSpec(memory_space=pltpu.VMEM)
    smem = pl.BlockSpec(memory_space=pltpu.SMEM)
    outs = pl.pallas_call(
        functools.partial(kernel, n_row, n_col),
        out_shape=(
            jax.ShapeDtypeStruct((tr, dl), BF16),
            jax.ShapeDtypeStruct((rank, dl), F32),
            jax.ShapeDtypeStruct((rank, fl), F32),
            jax.ShapeDtypeStruct((1, 1), F32),
        ),
        in_specs=[hbm, hbm, hbm, hbm, smem, hbm, hbm, smem, smem],
        out_specs=(vmem, vmem, vmem, smem),
        scratch_shapes=[
            pltpu.VMEM((tr, dl), BF16),
            pltpu.VMEM((2 * tr, fl), BF16),
            pltpu.VMEM((2 * tr, fl), BF16),
            pltpu.VMEM((fl, dl), BF16),
            pltpu.VMEM((rank, dl), F32),
            pltpu.VMEM((rank, fl), F32),
            pltpu.VMEM((n_col, SUB, 2 * tr // SUB, fl), BF16),
            pltpu.VMEM((fl, dl), BF16),
            pltpu.VMEM((n_chip, 4, 16, 128), F32),
            pltpu.VMEM((groups, n_chip, 4, 16, 128), BF16),
            pltpu.VMEM((groups, n_chip, 4, 16, 128), BF16),
            pltpu.VMEM((groups, n_chip, 4, 16, 128), BF16),
            pltpu.VMEM((groups, n_chip, 4, 16, 128), BF16),
            pltpu.VMEM((groups, 4, 16, 128), BF16),
            pltpu.VMEM((n_chip, 2, 16, 128), BF16),
            pltpu.VMEM((tr, dl), F32),
            pltpu.VMEM((rank // 16, 16, tr), BF16),
            pltpu.VMEM((n_col, 16, tr), BF16),
            pltpu.VMEM((n_row, rank // 16, 16, tr), BF16),
            pltpu.VMEM((n_col, rank, 2 * tr), BF16),
            pltpu.VMEM((n_col, rank, fl), F32),
            pltpu.VMEM((2 * n_pc, 8, tr), F32),
            pltpu.VMEM((n_row, 8, tr), F32),
            pltpu.VMEM((8, tr), F32),
            pltpu.VMEM((n_pc, 8, tr), F32),
            pltpu.VMEM((n_row, 8, 128), F32),
            pltpu.VMEM((n_row, 8, 128), F32),
            pltpu.VMEM((n_row, 8, 128), F32),
            pltpu.VMEM((n_col, 1, 128), F32),
            pltpu.SemaphoreType.DMA((2 * SUB + 4,)),
            pltpu.SemaphoreType.DMA((2, half, SUB)),
            pltpu.SemaphoreType.DMA((2, half, SUB)),
            pltpu.SemaphoreType.DMA((groups,)),
            pltpu.SemaphoreType.DMA((groups,)),
            pltpu.SemaphoreType.DMA((groups,)),
            pltpu.SemaphoreType.DMA((groups,)),
            pltpu.SemaphoreType.DMA((10,)),
            pltpu.SemaphoreType.DMA((10,)),
        ],
        compiler_params=pltpu.CompilerParams(
            collective_id=0, has_side_effects=True, vmem_limit_bytes=56 * 1024 * 1024
        ),
    )(
        tokens,
        gate_pre,
        grad_hidden,
        up_values,
        up_scales.T,
        adapter_down.T,
        adapter_up,
        layer_gates,
        layer,
    )
    grad_input, grad_down, grad_up, gate_grad = outs
    return grad_input, grad_down.T, grad_up, gate_grad.reshape(())


def solution(mesh):
    placed = (
        P("row", "col"),
        P("col", "row"),
        P("col", "row"),
        P("row", "col"),
        P("row", "col"),
        P("col", None),
        P(None, "row"),
        P(),
        P(),
    )
    return jax.shard_map(
        functools.partial(per_device, mesh.shape["row"], mesh.shape["col"]),
        mesh=mesh,
        in_specs=placed,
        out_specs=(P("row", "col"), P("col", None), P(None, "row"), P()),
        check_vma=False,
    )
```

```python
import functools

import jax
import jax.numpy as jnp
from jax import lax
from jax.experimental import pallas as pl
from jax.experimental.pallas import tpu as pltpu
from jax.sharding import PartitionSpec as P

QBLOCK = 128
SUB = 4
MESH = pl.DeviceIdType.MESH
F32 = jnp.float32
BF16 = jnp.bfloat16
Z1, Z2, Z3, Y1, Y2, YP, Y3, D1, D2, S1, FIN = range(11)


def split_rows(v):
    high = v.astype(BF16)
    low = (v - high.astype(F32)).astype(BF16)
    return jnp.concatenate([high, low], axis=0)


def fold_rows(v):
    half = v.shape[0] // 2
    return v[:half] + v[half:]


def dot_nt(a, b):
    return lax.dot_general(a, b, (((1,), (1,)), ((), ())), preferred_element_type=F32)


def dot_nn(a, b):
    return jnp.dot(a, b, preferred_element_type=F32)


def each(low, high, fn):
    def body(i, carry):
        fn(i)
        return carry

    lax.fori_loop(low, high, body, 0)


def kernel(
    n_row,
    n_col,
    tok_hbm,
    gate_hbm,
    hid_hbm,
    up_hbm,
    scale_hbm,
    down_hbm,
    adup_hbm,
    gates_hbm,
    layer_hbm,
    gi_ref,
    gd_ref,
    gu_ref,
    gg_ref,
    tok,
    gate,
    hid,
    up,
    a_t,
    adup,
    scale_ref,
    gates_ref,
    layer_ref,
    gbuf,
    wbuf,
    keep,
    xst,
    xrb,
    stage,
    rbuf,
    ost,
    fin,
    lora,
    zst,
    zrb,
    zfull,
    zcat,
    gpart,
    yst,
    yrb,
    y2st,
    yall,
    yt,
    gst,
    grb,
    gfull,
    srb,
    load_sem,
    ring_send,
    ring_recv,
    x_send,
    x_recv,
    rs_send,
    rs_recv,
    sm_send,
    sm_recv,
    next_sem,
    col_sem,
    row0_sem,
):
    r = lax.axis_index("row")
    c = lax.axis_index("col")
    core = lax.rem(r, 2)
    chip = lax.div(r, 2)
    tr, dl = gi_ref.shape
    fl = wbuf.shape[0]
    rank = gd_ref.shape[0]
    sub = 2 * tr // SUB
    n_pc = rank // 8
    n_chip = n_row // 2
    half = n_col // 2
    cgs = dl // 128
    tgs = n_chip // cgs
    right = lax.rem(c + 1, n_col)
    left = lax.rem(c + n_col - 1, n_col)
    odd = core == 1
    n_zp = rank // 16
    z_gap = n_col // n_zp
    z_owner = lax.rem(c, z_gap) == 0
    y_owner = lax.rem(c, 2) == 0
    my_z, my_k = lax.div(c, z_gap), lax.div(c, 2)

    def rcopy(src, dst, ssem, rsem, dev):
        return pltpu.make_async_remote_copy(
            src_ref=src, dst_ref=dst, send_sem=ssem, recv_sem=rsem, device_id=dev, device_id_type=MESH
        )

    def small(src, dst, which, dev):
        return rcopy(src, dst, sm_send.at[which], sm_recv.at[which], dev)

    def wait_small(which, ref):
        small(ref, ref, which, (r, right)).wait_recv()

    def sent(which, ref):
        small(ref, ref, which, (r, right)).wait_send()

    def plane_peer(i):
        return (lax.rem(r + i, n_row), c)

    def col_peer(i):
        return (r, lax.rem(c + i, n_col))

    barrier = pltpu.get_barrier_semaphore()
    first = c == 0

    def turn(i):
        late = jnp.where(i >= n_col - n_col // 4, half + n_col - 1 - i, i + n_col // 4)
        return jnp.where(i < half, i, late)

    my_turn = turn(c)
    right_later, left_later = turn(right) > my_turn, turn(left) > my_turn

    def hello(dev, sem=barrier):
        pl.semaphore_signal(sem, inc=1, device_id=dev, device_id_type=MESH)

    each(0, n_col, lambda i: pl.when(turn(i) > my_turn)(lambda: hello((r, i))))

    @pl.when(r > 0)
    def _():
        each(1, n_row, lambda i: hello(plane_peer(i)))

    def past_barrier():
        pl.when(r > 0)(lambda: pl.semaphore_wait(barrier, my_turn + n_row - 2))

        @pl.when(r == 0)
        def _():
            pl.semaphore_wait(barrier, my_turn + n_row - 1)
            each(1, n_row, lambda i: hello((i, c), row0_sem))

        pl.when(jnp.logical_not(left_later))(lambda: hello((r, left), next_sem.at[0]))
        pl.when(jnp.logical_not(right_later))(lambda: hello((r, right), next_sem.at[1]))
        each(0, n_col, lambda i: pl.when(turn(i) < my_turn)(lambda: hello((r, i), col_sem)))

    def neighbours_in():
        pl.when(right_later)(lambda: pl.semaphore_wait(next_sem.at[0], 1))
        pl.when(jnp.logical_and(left_later, c > 0))(lambda: pl.semaphore_wait(next_sem.at[1], 1))

    def rows(q):
        return pl.ds(q * sub, sub)

    loads = []
    for q in range(SUB):
        for at, (src, dst) in enumerate(((gate_hbm, gate), (hid_hbm, hid))):
            loads.append(pltpu.make_async_copy(src.at[rows(q)], dst.at[rows(q)], load_sem.at[2 * q + at]))
    others = (
        (tok_hbm, tok),
        (down_hbm, a_t),
        (adup_hbm, adup),
        (up_hbm, up),
        (scale_hbm, scale_ref),
        (gates_hbm, gates_ref),
        (layer_hbm, layer_ref),
    )
    for at, (src, dst) in enumerate(others):
        loads.append(pltpu.make_async_copy(src, dst, load_sem.at[2 * SUB + at]))
    for load in loads:
        load.start()

    def ring(way, s, h):
        if way == 0:
            block, dev = lax.rem(c - s + n_col, n_col), (r, right)
        else:
            block, dev = lax.rem(c + s, n_col), (r, left)
        part = gbuf.at[block, h]
        return rcopy(part, part, ring_send.at[way, s, h], ring_recv.at[way, s, h], dev)

    past_barrier()
    for q in range(SUB):
        loads[2 * q].wait()
        loads[2 * q + 1].wait()
        v = gate[rows(q), :].astype(F32)
        gbuf[c, q] = (hid[rows(q), :].astype(F32) * (v / (1.0 + jnp.exp(-v)))).astype(BF16)
        if q == 0:
            neighbours_in()
        ring(0, 0, q).start()
        pl.when(jnp.logical_not(first))(lambda: ring(1, 0, q).start())

    for load in loads[2 * SUB :]:
        load.wait()
    gv = gates_ref[layer_ref[0]]

    zst[...] = fold_rows(dot_nt(split_rows(a_t[...]), tok[...])).astype(BF16).reshape(n_zp, 16, tr)

    y_part = fold_rows(dot_nt(split_rows(adup[...]), gbuf[c].reshape(2 * tr, fl)))
    for k in range(n_pc):
        for h in range(2):
            yst[2 * k + h] = y_part[8 * k : 8 * k + 8, h * tr : (h + 1) * tr]

    def y1(i):
        @pl.when(2 * i + 1 != r)
        def _():
            small(yst.at[i], yrb.at[r], Y1, (2 * i + 1, c)).start()

    each(0, 2 * n_pc, y1)

    @pl.when(first)
    def _():
        pl.semaphore_wait(next_sem.at[1], 1)
        for q in range(SUB):
            ring(1, 0, q).start()


    def blocks_of(s):
        return (lax.rem(c - s + n_col, n_col), lax.rem(c + s, n_col))

    def tiles(v, put):
        for t in range(v.shape[0] // 16):
            for cg in range(cgs):
                put((t % tgs) * cgs + cg, t // tgs, v[16 * t : 16 * t + 16, 128 * cg : 128 * cg + 128])

    def multiply(group, parts, ours, theirs):
        def put_theirs(owner, at, v):
            xst[group, owner, at] = v.astype(BF16)

        def put_ours(owner, at, v):
            keep[owner, at] = v

        tiles(dot_nn(theirs, wbuf[...]), put_theirs)
        out, into = xst.at[group, :, pl.ds(0, parts)], xrb.at[group, :, pl.ds(0, parts)]
        rcopy(out, into, x_send.at[group], x_recv.at[group], (r + 1 - 2 * core, c)).start()
        tiles(dot_nn(ours, wbuf[...]), put_ours)

    def halves(block):
        def one(h):
            return jnp.concatenate([gbuf[block, 2 * h], gbuf[block, 2 * h + 1]], axis=0)

        return one(core), one(1 - core)

    def multiply_pair(s):
        ups, downs = blocks_of(s)
        up_ours, up_theirs = halves(ups)
        down_ours, down_theirs = halves(downs)
        multiply(
            s,
            4,
            jnp.concatenate([up_ours, down_ours], axis=0),
            jnp.concatenate([up_theirs, down_theirs], axis=0),
        )

    def scatter(group, parts):
        into = xrb.at[group, :, pl.ds(0, parts)]
        rcopy(into, into, x_send.at[group], x_recv.at[group], (r + 1 - 2 * core, c)).wait_recv()

        def add(p):
            both = keep[p, pl.ds(0, parts)] + xrb[group, p, pl.ds(0, parts)].astype(F32)
            stage[group, p, pl.ds(0, parts)] = both.astype(BF16)

        each(0, n_chip, add)

        def send(i):
            p = lax.rem(chip + i, n_chip)
            rcopy(
                stage.at[group, p, pl.ds(0, parts)],
                rbuf.at[group, chip, pl.ds(0, parts)],
                rs_send.at[group],
                rs_recv.at[group],
                (2 * p + core, c),
            ).start()

        each(1, n_chip, send)
        rbuf[group, chip, pl.ds(0, parts)] = stage[group, chip, pl.ds(0, parts)]

    def reduce(group, parts, pieces):
        got = rbuf.at[group, pl.ds(0, n_chip - 1), pl.ds(0, parts)]
        rcopy(got, got, rs_send.at[group], rs_recv.at[group], (r, right)).wait_recv()

        def add(i, acc):
            return acc + rbuf[group, i, pl.ds(0, parts)].astype(F32)

        total = lax.fori_loop(0, n_chip, add, jnp.zeros((parts, 16, 128), F32))
        ost[group, pl.ds(0, parts)] = total.astype(BF16)
        for at, size, block, place in pieces:

            @pl.when(block != chip)
            def _():
                small(
                    ost.at[group, pl.ds(at, size)],
                    fin.at[chip, pl.ds(place, size)],
                    FIN,
                    (2 * block + core, c),
                ).start()

            @pl.when(block == chip)
            def _():
                fin[chip, pl.ds(place, size)] = ost[group, pl.ds(at, size)]

    def reduce_pair(s):
        ups, downs = blocks_of(s)
        reduce(s, 4, ((0, 2, ups, 0), (2, 2, downs, 0)))

    def weights_and_own():
        pl.when(r > 0)(lambda: pl.semaphore_wait(row0_sem, 1))
        for i in range(fl // QBLOCK):
            for j in range(dl // QBLOCK):
                at = (pl.ds(i * QBLOCK, QBLOCK), pl.ds(j * QBLOCK, QBLOCK))
                wbuf[at] = (up[at].astype(F32) * scale_ref[j, i]).astype(BF16)
        ours, theirs = halves(c)
        multiply(0, 2, ours, theirs)

    def to_column(ref, which):
        each(1, n_col, lambda i: small(ref, ref, which, col_peer(i)).start())

    def wait_pieces(which, owner, count, ref):
        @pl.when(owner)
        def _():
            if count > 1:
                wait_small(which, ref.at[pl.ds(0, count - 1)])

        pl.when(jnp.logical_not(owner))(lambda: wait_small(which, ref))

    def z1(k):
        @pl.when(z_gap * k != c)
        def _():
            small(zst.at[k], zrb.at[c], Z1, (r, z_gap * k)).start()

    def z_start():
        pl.when(my_turn < n_col - 1)(lambda: pl.semaphore_wait(col_sem, n_col - 1 - my_turn))
        each(0, n_zp, z1)

    def z_sum():
        @pl.when(z_owner)
        def _():
            zrb[c] = zst[my_z]
            wait_small(Z1, zrb.at[pl.ds(0, n_col - 1)])
            zfull[r, my_z] = jnp.sum(zrb[...].astype(F32), axis=0).astype(BF16)
            to_column(zfull.at[r, my_z], Z2)

    def z_plane():
        wait_pieces(Z2, z_owner, n_zp, zfull.at[r])
        each(1, n_row, lambda i: small(zfull.at[r], zfull.at[r], Z3, plane_peer(i)).start())

    def z_ready():
        wait_small(Z3, zfull.at[pl.ds(0, n_row - 1)])

        def join(b):
            zcat[b] = jnp.concatenate(
                [zfull[2 * b].reshape(rank, tr), zfull[2 * b + 1].reshape(rank, tr)], axis=1
            )

        each(0, n_col, join)

    def y_sum():
        @pl.when(odd)
        def _():
            yrb[r] = yst[chip]
            wait_small(Y1, yrb.at[pl.ds(0, n_row - 1)])
            y2st[...] = jnp.sum(yrb[...], axis=0)
            k = lax.div(chip, 2)
            dest = 2 * c + lax.rem(chip, 2)

            @pl.when(dest != r)
            def _():
                small(y2st, yall.at[k], Y2, (dest, c)).start()

            @pl.when(dest == r)
            def _():
                yall[k] = y2st[...]

    def y_root():
        @pl.when(chip == c)
        def _():
            @pl.when(lax.rem(r, 4) == 3)
            def _():
                if n_pc > 1:
                    wait_small(Y2, yall.at[pl.ds(0, n_pc - 1)])

            pl.when(lax.rem(r, 4) != 3)(lambda: wait_small(Y2, yall))

            def part(k):
                @pl.when(2 * k != c)
                def _():
                    small(yall.at[k], yt.at[k], YP, (r, 2 * k)).start()

                @pl.when(2 * k == c)
                def _():
                    yt[k] = yall[k]

            each(0, n_pc, part)

    def y_column():
        @pl.when(y_owner)
        def _():
            pl.when(chip != c)(lambda: wait_small(YP, yt.at[my_k]))
            to_column(yt.at[my_k], Y3)

    def up_block(b):
        gpart[b] = dot_nn(zcat[b], gbuf[b].reshape(2 * tr, fl))

    def down_part():
        wait_pieces(Y3, y_owner, n_pc, yt)
        gd_t = fold_rows(dot_nn(split_rows(yt[...].reshape(rank, tr)), tok[...]))
        for k in range(n_pc):
            for q in range(cgs):
                gst[k * cgs + q] = gd_t[8 * k : 8 * k + 8, 128 * q : 128 * q + 128]

        def send(i):
            j = lax.rem(r + i, n_row)
            small(gst.at[j], grb.at[r], D1, (j, c)).start()

        each(1, n_row, send)
        grb[r] = gst[r]

    def make_lora():
        y_s = split_rows(yt[...].reshape(rank, tr))
        a_s = split_rows(a_t[...])
        y_left = jnp.concatenate([y_s[:rank], y_s[:rank], y_s[rank:]], axis=0).astype(F32).T.astype(BF16)
        a_right = jnp.concatenate([a_s[:rank], a_s[rank:], a_s[:rank]], axis=0)
        lora[...] = gv * dot_nn(y_left, a_right)

    def down_sum():
        wait_small(D1, grb.at[pl.ds(0, n_row - 1)])
        gfull[r] = jnp.sum(grb[...], axis=0)
        each(1, n_row, lambda i: small(gfull.at[r], gfull.at[r], D2, plane_peer(i)).start())

    def down_ready():
        wait_small(D2, gfull.at[pl.ds(0, n_row - 1)])
        strips = []
        for k in range(n_pc):
            strips.append(jnp.concatenate([gfull[k * cgs + q] for q in range(cgs)], axis=1))
        gd_t = jnp.concatenate(strips, axis=0)
        gd_ref[...] = gv * gd_t
        srb[c] = jnp.full(srb.shape[1:], jnp.sum(gd_t * a_t[...]), F32)

        to_column_gate()

    def to_column_gate():
        each(1, n_col, lambda i: small(srb.at[c], srb.at[c], S1, col_peer(i)).start())

    def gate_done():
        wait_small(S1, srb.at[pl.ds(0, n_col - 1)])
        gg_ref[0, 0] = jnp.sum(jnp.sum(srb[...], axis=0)[:, 0:1])

    up_at = 24

    def work(n):
        s, h = 1 + lax.div(n, SUB), lax.rem(n, SUB)
        pl.when(n == 0)(weights_and_own)
        @pl.when(jnp.logical_and(h == 1, s < half))
        def _():
            pl.when(s == 1)(lambda: scatter(0, 2))
            pl.when(s > 1)(lambda: scatter(s - 1, 4))

        @pl.when(jnp.logical_and(h == 0, jnp.logical_and(s > 1, s < half)))
        def _():
            pl.when(s == 2)(lambda: reduce(0, 2, ((0, 2, c, 0),)))
            pl.when(s > 2)(lambda: reduce_pair(s - 2))

        @pl.when(jnp.logical_and(h == 3, s < half))
        def _():
            multiply_pair(s)

        pl.when(n == 2)(y_sum)
        pl.when(n == 5)(z_start)
        pl.when(n == 5)(y_root)
        pl.when(n == 13)(z_sum)
        pl.when(n == 11)(y_column)
        pl.when(n == 20)(z_plane)
        pl.when(n == 18)(down_part)
        pl.when(n == 19)(make_lora)
        pl.when(n == 23)(z_ready)
        pl.when(n == 22)(down_sum)
        pl.when(n == 26)(down_ready)

        @pl.when(jnp.logical_and(n >= up_at, n < up_at + half // 2))
        def _():
            def group(i):
                ups, downs = blocks_of(2 * (n - up_at) + i)
                up_block(ups)
                pl.when(n + i > up_at)(lambda: up_block(downs))

            each(0, 2, group)

    def brings(way, h, at):
        split = jnp.where(at == 0, 0, SUB // 2)
        return h < split if way == 0 else h >= split

    def sends(way, h):
        return brings(way, h, right if way == 0 else left)

    def slot(n):
        s, h = 1 + lax.div(n, SUB), lax.rem(n, SUB)
        ring(0, s - 1, h).wait_recv()
        pl.when(jnp.logical_or(s < half - 1, sends(0, h)))(lambda: ring(0, s, h).start())
        ring(1, s - 1, h).wait_recv()
        pl.when(jnp.logical_or(s < half - 1, sends(1, h)))(lambda: ring(1, s, h).start())
        work(n)

    slots = SUB * (half - 1)
    each(0, slots, slot)
    last = up_at + 8
    if last > slots:
        each(slots, last, work)

    far = lax.rem(c + half, n_col)
    scatter(half - 1, 4)
    reduce_pair(half - 2)
    for t in range(2):
        for h in (t, t + 2):
            pl.when(brings(0, h, c))(lambda: ring(0, half - 1, h).wait_recv())
            pl.when(brings(1, h, c))(lambda: ring(1, half - 1, h).wait_recv())
        multiply(half + t, 1, gbuf[far, 2 * core + t], gbuf[far, 2 - 2 * core + t])
        scatter(half + t, 1)
    up_block(far)
    reduce_pair(half - 1)
    reduce(half, 1, ((0, 1, far, 0),))
    acc = gpart[0]
    for b in range(1, n_col):
        acc = acc + gpart[b]
    gu_ref[...] = gv * acc
    def drain(s):
        for way in range(2):
            for h in range(SUB):
                pl.when(jnp.logical_or(s < half - 1, sends(way, h)))(lambda: ring(way, s, h).wait_send())

    each(0, half, drain)

    def sent_group(group, parts):
        out = xst.at[group, :, pl.ds(0, parts)]
        rcopy(out, out, x_send.at[group], x_recv.at[group], (r, right)).wait_send()
        out = stage.at[group, pl.ds(0, n_chip - 1), pl.ds(0, parts)]
        rcopy(out, out, rs_send.at[group], rs_recv.at[group], (r, right)).wait_send()

    sent_group(0, 2)
    each(1, half, lambda s: sent_group(s, 4))
    sent_group(half, 1)

    @pl.when(odd)
    def _():
        sent(Y1, yst.at[pl.ds(0, 2 * n_pc - 1)])
        dest = 2 * c + lax.rem(chip, 2)
        pl.when(dest != r)(lambda: sent(Y2, y2st))

    @pl.when(chip == c)
    def _():
        @pl.when(y_owner)
        def _():
            if n_pc > 1:
                sent(YP, yall.at[pl.ds(0, n_pc - 1)])

        pl.when(jnp.logical_not(y_owner))(lambda: sent(YP, yall))

    pl.when(jnp.logical_not(odd))(lambda: sent(Y1, yst))

    @pl.when(z_owner)
    def _():
        if n_zp > 1:
            sent(Z1, zst.at[pl.ds(0, n_zp - 1)])
        sent(Z2, zrb.at[pl.ds(0, n_col - 1)])

    pl.when(jnp.logical_not(z_owner))(lambda: sent(Z1, zst))
    pl.when(y_owner)(lambda: sent(Y3, yrb.at[pl.ds(0, n_col - 1)]))
    sent(S1, srb.at[pl.ds(0, n_col - 1)])
    sent(Z3, zfull.at[pl.ds(0, n_row - 1)])
    sent(D1, gst.at[pl.ds(0, n_row - 1)])
    sent(D2, gfull.at[pl.ds(0, n_row - 1)])

    reduce(half + 1, 1, ((0, 1, far, 1),))
    wait_small(FIN, fin.at[pl.ds(0, n_chip - 1)])
    for p in range(n_chip):
        for at in range(2):
            here = (pl.ds(16 * (tgs * at + p // cgs), 16), pl.ds(128 * (p % cgs), 128))
            gi_ref[here] = (fin[p, at].astype(F32) + lora[here]).astype(BF16)
    gate_done()
    sent_group(half + 1, 1)
    sent(FIN, fin.at[pl.ds(0, n_chip - 1)])


def per_device(
    n_row,
    n_col,
    tokens,
    gate_pre,
    grad_hidden,
    up_values,
    up_scales,
    adapter_down,
    adapter_up,
    layer_gates,
    layer,
):
    tr, dl = tokens.shape
    fl = up_values.shape[0]
    rank = adapter_down.shape[1]
    n_pc = rank // 8
    n_chip = n_row // 2
    half = n_col // 2
    groups = half + 2
    hbm = pl.BlockSpec(memory_space=pltpu.HBM)
    vmem = pl.BlockSpec(memory_space=pltpu.VMEM)
    smem = pl.BlockSpec(memory_space=pltpu.SMEM)
    outs = pl.pallas_call(
        functools.partial(kernel, n_row, n_col),
        out_shape=(
            jax.ShapeDtypeStruct((tr, dl), BF16),
            jax.ShapeDtypeStruct((rank, dl), F32),
            jax.ShapeDtypeStruct((rank, fl), F32),
            jax.ShapeDtypeStruct((1, 1), F32),
        ),
        in_specs=[hbm] * 9,
        out_specs=(vmem, vmem, vmem, smem),
        scratch_shapes=[
            pltpu.VMEM((tr, dl), BF16),
            pltpu.VMEM((2 * tr, fl), BF16),
            pltpu.VMEM((2 * tr, fl), BF16),
            pltpu.VMEM((fl, dl), BF16),
            pltpu.VMEM((rank, dl), F32),
            pltpu.VMEM((rank, fl), F32),
            pltpu.SMEM((dl // QBLOCK, fl // QBLOCK), F32),
            pltpu.SMEM(layer_gates.shape, F32),
            pltpu.SMEM((1,), jnp.int32),
            pltpu.VMEM((n_col, SUB, 2 * tr // SUB, fl), BF16),
            pltpu.VMEM((fl, dl), BF16),
            pltpu.VMEM((n_chip, 4, 16, 128), F32),
            pltpu.VMEM((groups, n_chip, 4, 16, 128), BF16),
            pltpu.VMEM((groups, n_chip, 4, 16, 128), BF16),
            pltpu.VMEM((groups, n_chip, 4, 16, 128), BF16),
            pltpu.VMEM((groups, n_chip, 4, 16, 128), BF16),
            pltpu.VMEM((groups, 4, 16, 128), BF16),
            pltpu.VMEM((n_chip, 2, 16, 128), BF16),
            pltpu.VMEM((tr, dl), F32),
            pltpu.VMEM((rank // 16, 16, tr), BF16),
            pltpu.VMEM((n_col, 16, tr), BF16),
            pltpu.VMEM((n_row, rank // 16, 16, tr), BF16),
            pltpu.VMEM((n_col, rank, 2 * tr), BF16),
            pltpu.VMEM((n_col, rank, fl), F32),
            pltpu.VMEM((2 * n_pc, 8, tr), F32),
            pltpu.VMEM((n_row, 8, tr), F32),
            pltpu.VMEM((8, tr), F32),
            pltpu.VMEM((n_pc, 8, tr), F32),
            pltpu.VMEM((n_pc, 8, tr), F32),
            pltpu.VMEM((n_row, 8, 128), F32),
            pltpu.VMEM((n_row, 8, 128), F32),
            pltpu.VMEM((n_row, 8, 128), F32),
            pltpu.VMEM((n_col, 1, 128), F32),
            pltpu.SemaphoreType.DMA((2 * SUB + 7,)),
            pltpu.SemaphoreType.DMA((2, half, SUB)),
            pltpu.SemaphoreType.DMA((2, half, SUB)),
            pltpu.SemaphoreType.DMA((groups,)),
            pltpu.SemaphoreType.DMA((groups,)),
            pltpu.SemaphoreType.DMA((groups,)),
            pltpu.SemaphoreType.DMA((groups,)),
            pltpu.SemaphoreType.DMA((11,)),
            pltpu.SemaphoreType.DMA((11,)),
            pltpu.SemaphoreType.REGULAR((2,)),
            pltpu.SemaphoreType.REGULAR,
            pltpu.SemaphoreType.REGULAR,
        ],
        compiler_params=pltpu.CompilerParams(
            collective_id=0, has_side_effects=True, vmem_limit_bytes=56 * 1024 * 1024
        ),
    )(
        tokens,
        gate_pre,
        grad_hidden,
        up_values,
        up_scales.T,
        adapter_down.T,
        adapter_up,
        layer_gates,
        layer,
    )
    grad_input, grad_down, grad_up, gate_grad = outs
    return grad_input, grad_down.T, grad_up, gate_grad.reshape(())


def solution(mesh):
    placed = (
        P("row", "col"),
        P("col", "row"),
        P("col", "row"),
        P("row", "col"),
        P("row", "col"),
        P("col", None),
        P(None, "row"),
        P(),
        P(),
    )
    return jax.shard_map(
        functools.partial(per_device, mesh.shape["row"], mesh.shape["col"]),
        mesh=mesh,
        in_specs=placed,
        out_specs=(P("row", "col"), P("col", None), P(None, "row"), P()),
        check_vma=False,
    )
```

```python
import functools

import jax
import jax.numpy as jnp
from jax import lax
from jax.experimental import pallas as pl
from jax.experimental.pallas import tpu as pltpu
from jax.sharding import PartitionSpec as P

QBLOCK = 128
SUB = 4
MESH = pl.DeviceIdType.MESH
F32 = jnp.float32
BF16 = jnp.bfloat16
Z1, Z2, Z3, Y1, Y2, YP, Y3, D1, D2, S1, FIN = range(11)


def split_rows(v):
    high = v.astype(BF16)
    low = (v - high.astype(F32)).astype(BF16)
    return jnp.concatenate([high, low], axis=0)


def fold_rows(v):
    half = v.shape[0] // 2
    return v[:half] + v[half:]


def dot_nt(a, b):
    return lax.dot_general(a, b, (((1,), (1,)), ((), ())), preferred_element_type=F32)


def dot_nn(a, b):
    return jnp.dot(a, b, preferred_element_type=F32)


def each(low, high, fn):
    def body(i, carry):
        fn(i)
        return carry

    lax.fori_loop(low, high, body, 0)


def kernel(
    n_row,
    n_col,
    tok_hbm,
    gate_hbm,
    hid_hbm,
    up_hbm,
    scale_hbm,
    down_hbm,
    adup_hbm,
    gates_hbm,
    layer_hbm,
    gi_ref,
    gd_hbm,
    gu_hbm,
    gg_ref,
    tok,
    gate,
    hid,
    up,
    a_t,
    adup,
    scale_ref,
    gates_ref,
    layer_ref,
    gbuf,
    wbuf,
    keep,
    xst,
    xrb,
    stage,
    rbuf,
    ost,
    fin,
    lora,
    zst,
    zrb,
    zfull,
    zcat,
    gpart,
    yst,
    yrb,
    y2st,
    yall,
    yt,
    gst,
    grb,
    gfull,
    srb,
    load_sem,
    ring_send,
    ring_recv,
    x_send,
    x_recv,
    rs_send,
    rs_recv,
    sm_send,
    sm_recv,
    next_sem,
    col_sem,
    row0_sem,
    gd_ref,
    gu_ref,
    out_sem,
):
    r = lax.axis_index("row")
    c = lax.axis_index("col")
    core = lax.rem(r, 2)
    chip = lax.div(r, 2)
    tr, dl = gi_ref.shape
    fl = wbuf.shape[0]
    rank = gd_hbm.shape[0]
    sub = 2 * tr // SUB
    n_pc = rank // 8
    n_chip = n_row // 2
    half = n_col // 2
    cgs = dl // 128
    tgs = n_chip // cgs
    right = lax.rem(c + 1, n_col)
    left = lax.rem(c + n_col - 1, n_col)
    odd = core == 1
    n_zp = rank // 16
    z_gap = n_col // n_zp
    z_owner = lax.rem(c, z_gap) == 0
    y_owner = lax.rem(c, 2) == 0
    my_z, my_k = lax.div(c, z_gap), lax.div(c, 2)

    gd_out = pltpu.make_async_copy(gd_ref, gd_hbm, out_sem.at[0])
    gu_out = pltpu.make_async_copy(gu_ref, gu_hbm, out_sem.at[1])

    def rcopy(src, dst, ssem, rsem, dev):
        return pltpu.make_async_remote_copy(
            src_ref=src, dst_ref=dst, send_sem=ssem, recv_sem=rsem, device_id=dev, device_id_type=MESH
        )

    def small(src, dst, which, dev):
        return rcopy(src, dst, sm_send.at[which], sm_recv.at[which], dev)

    def wait_small(which, ref):
        small(ref, ref, which, (r, right)).wait_recv()

    def sent(which, ref):
        small(ref, ref, which, (r, right)).wait_send()

    def plane_peer(i):
        return (lax.rem(r + i, n_row), c)

    def col_peer(i):
        return (r, lax.rem(c + i, n_col))

    barrier = pltpu.get_barrier_semaphore()
    first = c == 0

    def turn(i):
        late = jnp.where(i >= n_col - n_col // 4, half + n_col - 1 - i, i + n_col // 4)
        return jnp.where(i < half, i, late)

    my_turn = turn(c)
    right_later, left_later = turn(right) > my_turn, turn(left) > my_turn

    def hello(dev, sem=barrier):
        pl.semaphore_signal(sem, inc=1, device_id=dev, device_id_type=MESH)

    each(0, n_col, lambda i: pl.when(turn(i) > my_turn)(lambda: hello((r, i))))

    @pl.when(r > 0)
    def _():
        each(1, n_row, lambda i: hello(plane_peer(i)))

    def past_barrier():
        pl.when(r > 0)(lambda: pl.semaphore_wait(barrier, my_turn + n_row - 2))

        @pl.when(r == 0)
        def _():
            pl.semaphore_wait(barrier, my_turn + n_row - 1)
            each(1, n_row, lambda i: hello((i, c), row0_sem))

        pl.when(jnp.logical_not(left_later))(lambda: hello((r, left), next_sem.at[0]))
        pl.when(jnp.logical_not(right_later))(lambda: hello((r, right), next_sem.at[1]))
        each(0, n_col, lambda i: pl.when(turn(i) < my_turn)(lambda: hello((r, i), col_sem)))

    def neighbours_in():
        pl.when(right_later)(lambda: pl.semaphore_wait(next_sem.at[0], 1))
        pl.when(jnp.logical_and(left_later, c > 0))(lambda: pl.semaphore_wait(next_sem.at[1], 1))

    def rows(q):
        return pl.ds(q * sub, sub)

    loads = []
    for q in range(SUB):
        for at, (src, dst) in enumerate(((gate_hbm, gate), (hid_hbm, hid))):
            loads.append(pltpu.make_async_copy(src.at[rows(q)], dst.at[rows(q)], load_sem.at[2 * q + at]))
    others = (
        (tok_hbm, tok),
        (down_hbm, a_t),
        (adup_hbm, adup),
        (up_hbm, up),
        (scale_hbm, scale_ref),
        (gates_hbm, gates_ref),
        (layer_hbm, layer_ref),
    )
    for at, (src, dst) in enumerate(others):
        loads.append(pltpu.make_async_copy(src, dst, load_sem.at[2 * SUB + at]))
    for load in loads:
        load.start()

    def ring(way, s, h):
        if way == 0:
            block, dev = lax.rem(c - s + n_col, n_col), (r, right)
        else:
            block, dev = lax.rem(c + s, n_col), (r, left)
        part = gbuf.at[block, h]
        return rcopy(part, part, ring_send.at[way, s, h], ring_recv.at[way, s, h], dev)

    past_barrier()
    for q in range(SUB):
        loads[2 * q].wait()
        loads[2 * q + 1].wait()
        v = gate[rows(q), :].astype(F32)
        gbuf[c, q] = (hid[rows(q), :].astype(F32) * (v / (1.0 + jnp.exp(-v)))).astype(BF16)
        if q == 0:
            neighbours_in()
        ring(0, 0, q).start()
        pl.when(jnp.logical_not(first))(lambda: ring(1, 0, q).start())

    for load in loads[2 * SUB :]:
        load.wait()
    gv = gates_ref[layer_ref[0]]

    zst[...] = fold_rows(dot_nt(split_rows(a_t[...]), tok[...])).astype(BF16).reshape(n_zp, 16, tr)

    y_part = fold_rows(dot_nt(split_rows(adup[...]), gbuf[c].reshape(2 * tr, fl)))
    for k in range(n_pc):
        for h in range(2):
            yst[2 * k + h] = y_part[8 * k : 8 * k + 8, h * tr : (h + 1) * tr]

    def y1(i):
        @pl.when(2 * i + 1 != r)
        def _():
            small(yst.at[i], yrb.at[r], Y1, (2 * i + 1, c)).start()

    each(0, 2 * n_pc, y1)

    @pl.when(first)
    def _():
        pl.semaphore_wait(next_sem.at[1], 1)
        for q in range(SUB):
            ring(1, 0, q).start()


    def blocks_of(s):
        return (lax.rem(c - s + n_col, n_col), lax.rem(c + s, n_col))

    def tiles(v, put):
        for t in range(v.shape[0] // 16):
            for cg in range(cgs):
                put((t % tgs) * cgs + cg, t // tgs, v[16 * t : 16 * t + 16, 128 * cg : 128 * cg + 128])

    def multiply(group, parts, ours, theirs):
        def put_theirs(owner, at, v):
            xst[group, owner, at] = v.astype(BF16)

        def put_ours(owner, at, v):
            keep[owner, at] = v

        tiles(dot_nn(theirs, wbuf[...]), put_theirs)
        out, into = xst.at[group, :, pl.ds(0, parts)], xrb.at[group, :, pl.ds(0, parts)]
        rcopy(out, into, x_send.at[group], x_recv.at[group], (r + 1 - 2 * core, c)).start()
        tiles(dot_nn(ours, wbuf[...]), put_ours)

    def halves(block):
        def one(h):
            return jnp.concatenate([gbuf[block, 2 * h], gbuf[block, 2 * h + 1]], axis=0)

        return one(core), one(1 - core)

    def multiply_pair(s):
        ups, downs = blocks_of(s)
        up_ours, up_theirs = halves(ups)
        down_ours, down_theirs = halves(downs)
        multiply(
            s,
            4,
            jnp.concatenate([up_ours, down_ours], axis=0),
            jnp.concatenate([up_theirs, down_theirs], axis=0),
        )

    def scatter(group, parts):
        into = xrb.at[group, :, pl.ds(0, parts)]
        rcopy(into, into, x_send.at[group], x_recv.at[group], (r + 1 - 2 * core, c)).wait_recv()

        def add(p):
            both = keep[p, pl.ds(0, parts)] + xrb[group, p, pl.ds(0, parts)].astype(F32)
            stage[group, p, pl.ds(0, parts)] = both.astype(BF16)

        each(0, n_chip, add)

        def send(i):
            p = lax.rem(chip + i, n_chip)
            rcopy(
                stage.at[group, p, pl.ds(0, parts)],
                rbuf.at[group, chip, pl.ds(0, parts)],
                rs_send.at[group],
                rs_recv.at[group],
                (2 * p + core, c),
            ).start()

        each(1, n_chip, send)
        rbuf[group, chip, pl.ds(0, parts)] = stage[group, chip, pl.ds(0, parts)]

    def reduce(group, parts, pieces):
        got = rbuf.at[group, pl.ds(0, n_chip - 1), pl.ds(0, parts)]
        rcopy(got, got, rs_send.at[group], rs_recv.at[group], (r, right)).wait_recv()

        def add(i, acc):
            return acc + rbuf[group, i, pl.ds(0, parts)].astype(F32)

        total = lax.fori_loop(0, n_chip, add, jnp.zeros((parts, 16, 128), F32))
        ost[group, pl.ds(0, parts)] = total.astype(BF16)
        for at, size, block, place in pieces:

            @pl.when(block != chip)
            def _():
                small(
                    ost.at[group, pl.ds(at, size)],
                    fin.at[chip, pl.ds(place, size)],
                    FIN,
                    (2 * block + core, c),
                ).start()

            @pl.when(block == chip)
            def _():
                fin[chip, pl.ds(place, size)] = ost[group, pl.ds(at, size)]

    def reduce_pair(s):
        ups, downs = blocks_of(s)
        reduce(s, 4, ((0, 2, ups, 0), (2, 2, downs, 0)))

    def weights_and_own():
        pl.when(r > 0)(lambda: pl.semaphore_wait(row0_sem, 1))
        for i in range(fl // QBLOCK):
            for j in range(dl // QBLOCK):
                at = (pl.ds(i * QBLOCK, QBLOCK), pl.ds(j * QBLOCK, QBLOCK))
                wbuf[at] = (up[at].astype(F32) * scale_ref[j, i]).astype(BF16)
        ours, theirs = halves(c)
        multiply(0, 2, ours, theirs)

    def to_column(ref, which):
        each(1, n_col, lambda i: small(ref, ref, which, col_peer(i)).start())

    def wait_pieces(which, owner, count, ref):
        @pl.when(owner)
        def _():
            if count > 1:
                wait_small(which, ref.at[pl.ds(0, count - 1)])

        pl.when(jnp.logical_not(owner))(lambda: wait_small(which, ref))

    def z1(k):
        @pl.when(z_gap * k != c)
        def _():
            small(zst.at[k], zrb.at[c], Z1, (r, z_gap * k)).start()

    def z_start():
        pl.when(my_turn < n_col - 1)(lambda: pl.semaphore_wait(col_sem, n_col - 1 - my_turn))
        each(0, n_zp, z1)

    def z_sum():
        @pl.when(z_owner)
        def _():
            zrb[c] = zst[my_z]
            wait_small(Z1, zrb.at[pl.ds(0, n_col - 1)])
            zfull[r, my_z] = jnp.sum(zrb[...].astype(F32), axis=0).astype(BF16)
            to_column(zfull.at[r, my_z], Z2)

    def z_plane():
        wait_pieces(Z2, z_owner, n_zp, zfull.at[r])
        each(1, n_row, lambda i: small(zfull.at[r], zfull.at[r], Z3, plane_peer(i)).start())

    def z_ready():
        wait_small(Z3, zfull.at[pl.ds(0, n_row - 1)])

        def join(b):
            zcat[b] = jnp.concatenate(
                [zfull[2 * b].reshape(rank, tr), zfull[2 * b + 1].reshape(rank, tr)], axis=1
            )

        each(0, n_col, join)

    def y_sum():
        @pl.when(odd)
        def _():
            yrb[r] = yst[chip]
            wait_small(Y1, yrb.at[pl.ds(0, n_row - 1)])
            y2st[...] = jnp.sum(yrb[...], axis=0)
            k = lax.div(chip, 2)
            dest = 2 * c + lax.rem(chip, 2)

            @pl.when(dest != r)
            def _():
                small(y2st, yall.at[k], Y2, (dest, c)).start()

            @pl.when(dest == r)
            def _():
                yall[k] = y2st[...]

    def y_root():
        @pl.when(chip == c)
        def _():
            @pl.when(lax.rem(r, 4) == 3)
            def _():
                if n_pc > 1:
                    wait_small(Y2, yall.at[pl.ds(0, n_pc - 1)])

            pl.when(lax.rem(r, 4) != 3)(lambda: wait_small(Y2, yall))

            def part(k):
                @pl.when(2 * k != c)
                def _():
                    small(yall.at[k], yt.at[k], YP, (r, 2 * k)).start()

                @pl.when(2 * k == c)
                def _():
                    yt[k] = yall[k]

            each(0, n_pc, part)

    def y_column():
        @pl.when(y_owner)
        def _():
            pl.when(chip != c)(lambda: wait_small(YP, yt.at[my_k]))
            to_column(yt.at[my_k], Y3)

    def up_block(b):
        gpart[b] = dot_nn(zcat[b], gbuf[b].reshape(2 * tr, fl))

    def down_part():
        wait_pieces(Y3, y_owner, n_pc, yt)
        gd_t = fold_rows(dot_nn(split_rows(yt[...].reshape(rank, tr)), tok[...]))
        for k in range(n_pc):
            for q in range(cgs):
                gst[k * cgs + q] = gd_t[8 * k : 8 * k + 8, 128 * q : 128 * q + 128]

        def send(i):
            j = lax.rem(r + i, n_row)
            small(gst.at[j], grb.at[r], D1, (j, c)).start()

        each(1, n_row, send)
        grb[r] = gst[r]

    def make_lora():
        y_s = split_rows(yt[...].reshape(rank, tr))
        a_s = split_rows(a_t[...])
        y_left = jnp.concatenate([y_s[:rank], y_s[:rank], y_s[rank:]], axis=0).astype(F32).T.astype(BF16)
        a_right = jnp.concatenate([a_s[:rank], a_s[rank:], a_s[:rank]], axis=0)
        lora[...] = gv * dot_nn(y_left, a_right)

    def down_sum():
        wait_small(D1, grb.at[pl.ds(0, n_row - 1)])
        gfull[r] = jnp.sum(grb[...], axis=0)
        each(1, n_row, lambda i: small(gfull.at[r], gfull.at[r], D2, plane_peer(i)).start())

    def down_ready():
        wait_small(D2, gfull.at[pl.ds(0, n_row - 1)])
        strips = []
        for k in range(n_pc):
            strips.append(jnp.concatenate([gfull[k * cgs + q] for q in range(cgs)], axis=1))
        gd_t = jnp.concatenate(strips, axis=0)
        gd_ref[...] = gv * gd_t
        gd_out.start()
        srb[c] = jnp.full(srb.shape[1:], jnp.sum(gd_t * a_t[...]), F32)

        to_column_gate()

    def to_column_gate():
        each(1, n_col, lambda i: small(srb.at[c], srb.at[c], S1, col_peer(i)).start())

    def gate_done():
        wait_small(S1, srb.at[pl.ds(0, n_col - 1)])
        gg_ref[0, 0] = jnp.sum(jnp.sum(srb[...], axis=0)[:, 0:1])

    up_at = 24

    def work(n):
        s, h = 1 + lax.div(n, SUB), lax.rem(n, SUB)
        pl.when(n == 0)(weights_and_own)
        @pl.when(jnp.logical_and(h == 1, s < half))
        def _():
            pl.when(s == 1)(lambda: scatter(0, 2))
            pl.when(s > 1)(lambda: scatter(s - 1, 4))

        @pl.when(jnp.logical_and(h == 0, jnp.logical_and(s > 1, s < half)))
        def _():
            pl.when(s == 2)(lambda: reduce(0, 2, ((0, 2, c, 0),)))
            pl.when(s > 2)(lambda: reduce_pair(s - 2))

        @pl.when(jnp.logical_and(h == 3, s < half))
        def _():
            multiply_pair(s)

        pl.when(n == 2)(y_sum)
        pl.when(n == 5)(z_start)
        pl.when(n == 5)(y_root)
        pl.when(n == 13)(z_sum)
        pl.when(n == 11)(y_column)
        pl.when(n == 20)(z_plane)
        pl.when(n == 18)(down_part)
        pl.when(n == 19)(make_lora)
        pl.when(n == 23)(z_ready)
        pl.when(n == 22)(down_sum)
        pl.when(n == 26)(down_ready)

        @pl.when(jnp.logical_and(n >= up_at, n < up_at + half // 2))
        def _():
            def group(i):
                ups, downs = blocks_of(2 * (n - up_at) + i)
                up_block(ups)
                pl.when(n + i > up_at)(lambda: up_block(downs))

            each(0, 2, group)

    def brings(way, h, at):
        split = jnp.where(at == 0, 0, SUB // 2)
        return h < split if way == 0 else h >= split

    def sends(way, h):
        return brings(way, h, right if way == 0 else left)

    def slot(n):
        s, h = 1 + lax.div(n, SUB), lax.rem(n, SUB)
        ring(0, s - 1, h).wait_recv()
        pl.when(jnp.logical_or(s < half - 1, sends(0, h)))(lambda: ring(0, s, h).start())
        ring(1, s - 1, h).wait_recv()
        pl.when(jnp.logical_or(s < half - 1, sends(1, h)))(lambda: ring(1, s, h).start())
        work(n)

    slots = SUB * (half - 1)
    each(0, slots, slot)
    last = up_at + 8
    if last > slots:
        each(slots, last, work)

    far = lax.rem(c + half, n_col)
    scatter(half - 1, 4)
    reduce_pair(half - 2)
    for t in range(2):
        for h in (t, t + 2):
            pl.when(brings(0, h, c))(lambda: ring(0, half - 1, h).wait_recv())
            pl.when(brings(1, h, c))(lambda: ring(1, half - 1, h).wait_recv())
        multiply(half + t, 1, gbuf[far, 2 * core + t], gbuf[far, 2 - 2 * core + t])
        scatter(half + t, 1)
    up_block(far)
    reduce_pair(half - 1)
    reduce(half, 1, ((0, 1, far, 0),))
    acc = gpart[0]
    for b in range(1, n_col):
        acc = acc + gpart[b]
    gu_ref[...] = gv * acc
    gu_out.start()
    def drain(s):
        for way in range(2):
            for h in range(SUB):
                pl.when(jnp.logical_or(s < half - 1, sends(way, h)))(lambda: ring(way, s, h).wait_send())

    each(0, half, drain)

    def sent_group(group, parts):
        out = xst.at[group, :, pl.ds(0, parts)]
        rcopy(out, out, x_send.at[group], x_recv.at[group], (r, right)).wait_send()
        out = stage.at[group, pl.ds(0, n_chip - 1), pl.ds(0, parts)]
        rcopy(out, out, rs_send.at[group], rs_recv.at[group], (r, right)).wait_send()

    sent_group(0, 2)
    each(1, half, lambda s: sent_group(s, 4))
    sent_group(half, 1)

    @pl.when(odd)
    def _():
        sent(Y1, yst.at[pl.ds(0, 2 * n_pc - 1)])
        dest = 2 * c + lax.rem(chip, 2)
        pl.when(dest != r)(lambda: sent(Y2, y2st))

    @pl.when(chip == c)
    def _():
        @pl.when(y_owner)
        def _():
            if n_pc > 1:
                sent(YP, yall.at[pl.ds(0, n_pc - 1)])

        pl.when(jnp.logical_not(y_owner))(lambda: sent(YP, yall))

    pl.when(jnp.logical_not(odd))(lambda: sent(Y1, yst))

    @pl.when(z_owner)
    def _():
        if n_zp > 1:
            sent(Z1, zst.at[pl.ds(0, n_zp - 1)])
        sent(Z2, zrb.at[pl.ds(0, n_col - 1)])

    pl.when(jnp.logical_not(z_owner))(lambda: sent(Z1, zst))
    pl.when(y_owner)(lambda: sent(Y3, yrb.at[pl.ds(0, n_col - 1)]))
    sent(S1, srb.at[pl.ds(0, n_col - 1)])
    sent(Z3, zfull.at[pl.ds(0, n_row - 1)])
    sent(D1, gst.at[pl.ds(0, n_row - 1)])
    sent(D2, gfull.at[pl.ds(0, n_row - 1)])

    reduce(half + 1, 1, ((0, 1, far, 1),))
    wait_small(FIN, fin.at[pl.ds(0, n_chip - 1)])
    for p in range(n_chip):
        for at in range(2):
            here = (pl.ds(16 * (tgs * at + p // cgs), 16), pl.ds(128 * (p % cgs), 128))
            gi_ref[here] = (fin[p, at].astype(F32) + lora[here]).astype(BF16)
    gate_done()
    sent_group(half + 1, 1)
    sent(FIN, fin.at[pl.ds(0, n_chip - 1)])
    gd_out.wait()
    gu_out.wait()


def per_device(
    n_row,
    n_col,
    tokens,
    gate_pre,
    grad_hidden,
    up_values,
    up_scales,
    adapter_down,
    adapter_up,
    layer_gates,
    layer,
):
    tr, dl = tokens.shape
    fl = up_values.shape[0]
    rank = adapter_down.shape[1]
    n_pc = rank // 8
    n_chip = n_row // 2
    half = n_col // 2
    groups = half + 2
    hbm = pl.BlockSpec(memory_space=pltpu.HBM)
    vmem = pl.BlockSpec(memory_space=pltpu.VMEM)
    smem = pl.BlockSpec(memory_space=pltpu.SMEM)
    outs = pl.pallas_call(
        functools.partial(kernel, n_row, n_col),
        out_shape=(
            jax.ShapeDtypeStruct((tr, dl), BF16),
            jax.ShapeDtypeStruct((rank, dl), F32),
            jax.ShapeDtypeStruct((rank, fl), F32),
            jax.ShapeDtypeStruct((1, 1), F32),
        ),
        in_specs=[hbm] * 9,
        out_specs=(vmem, hbm, hbm, smem),
        scratch_shapes=[
            pltpu.VMEM((tr, dl), BF16),
            pltpu.VMEM((2 * tr, fl), BF16),
            pltpu.VMEM((2 * tr, fl), BF16),
            pltpu.VMEM((fl, dl), BF16),
            pltpu.VMEM((rank, dl), F32),
            pltpu.VMEM((rank, fl), F32),
            pltpu.SMEM((dl // QBLOCK, fl // QBLOCK), F32),
            pltpu.SMEM(layer_gates.shape, F32),
            pltpu.SMEM((1,), jnp.int32),
            pltpu.VMEM((n_col, SUB, 2 * tr // SUB, fl), BF16),
            pltpu.VMEM((fl, dl), BF16),
            pltpu.VMEM((n_chip, 4, 16, 128), F32),
            pltpu.VMEM((groups, n_chip, 4, 16, 128), BF16),
            pltpu.VMEM((groups, n_chip, 4, 16, 128), BF16),
            pltpu.VMEM((groups, n_chip, 4, 16, 128), BF16),
            pltpu.VMEM((groups, n_chip, 4, 16, 128), BF16),
            pltpu.VMEM((groups, 4, 16, 128), BF16),
            pltpu.VMEM((n_chip, 2, 16, 128), BF16),
            pltpu.VMEM((tr, dl), F32),
            pltpu.VMEM((rank // 16, 16, tr), BF16),
            pltpu.VMEM((n_col, 16, tr), BF16),
            pltpu.VMEM((n_row, rank // 16, 16, tr), BF16),
            pltpu.VMEM((n_col, rank, 2 * tr), BF16),
            pltpu.VMEM((n_col, rank, fl), F32),
            pltpu.VMEM((2 * n_pc, 8, tr), F32),
            pltpu.VMEM((n_row, 8, tr), F32),
            pltpu.VMEM((8, tr), F32),
            pltpu.VMEM((n_pc, 8, tr), F32),
            pltpu.VMEM((n_pc, 8, tr), F32),
            pltpu.VMEM((n_row, 8, 128), F32),
            pltpu.VMEM((n_row, 8, 128), F32),
            pltpu.VMEM((n_row, 8, 128), F32),
            pltpu.VMEM((n_col, 1, 128), F32),
            pltpu.SemaphoreType.DMA((2 * SUB + 7,)),
            pltpu.SemaphoreType.DMA((2, half, SUB)),
            pltpu.SemaphoreType.DMA((2, half, SUB)),
            pltpu.SemaphoreType.DMA((groups,)),
            pltpu.SemaphoreType.DMA((groups,)),
            pltpu.SemaphoreType.DMA((groups,)),
            pltpu.SemaphoreType.DMA((groups,)),
            pltpu.SemaphoreType.DMA((11,)),
            pltpu.SemaphoreType.DMA((11,)),
            pltpu.SemaphoreType.REGULAR((2,)),
            pltpu.SemaphoreType.REGULAR,
            pltpu.SemaphoreType.REGULAR,
            pltpu.VMEM((rank, dl), F32),
            pltpu.VMEM((rank, fl), F32),
            pltpu.SemaphoreType.DMA((2,)),
        ],
        compiler_params=pltpu.CompilerParams(
            collective_id=0, has_side_effects=True, vmem_limit_bytes=56 * 1024 * 1024
        ),
    )(
        tokens,
        gate_pre,
        grad_hidden,
        up_values,
        up_scales.T,
        adapter_down.T,
        adapter_up,
        layer_gates,
        layer,
    )
    grad_input, grad_down, grad_up, gate_grad = outs
    return grad_input, grad_down.T, grad_up, gate_grad.reshape(())


def solution(mesh):
    placed = (
        P("row", "col"),
        P("col", "row"),
        P("col", "row"),
        P("row", "col"),
        P("row", "col"),
        P("col", None),
        P(None, "row"),
        P(),
        P(),
    )
    return jax.shard_map(
        functools.partial(per_device, mesh.shape["row"], mesh.shape["col"]),
        mesh=mesh,
        in_specs=placed,
        out_specs=(P("row", "col"), P("col", None), P(None, "row"), P()),
        check_vma=False,
    )
```
